256 devices in a mesh: store: 8 (over x, y_hi), tensor: 32 (over z, y_lo, core).
Axes of the slice: x: 4, y: 4 (y_hi: 2, y_lo: 2; y = y_hi * 2 + y_lo), z: 8, core: 2. Of those that a mesh axis runs over, the one named last changes fastest.
Arguments:
- suffix_tokens: bfloat16 [4096, 8192], P(('store', 'tensor')), may hold values from -6 to 6
- q_weight: bfloat16 [8192, 8192], P(None, 'tensor'), may hold values from -0.125 to 0.125
- kv_weight: bfloat16 [8192, 32, 8, 8], P(None, 'tensor'), may hold values from -0.0625 to 0.0625
- out_weight: bfloat16 [8192, 8192], P('tensor'), may hold values from -0.375 to 0.375
- prefix_pool: bfloat16 [8, 256, 8, 16, 256], P('store', 'tensor'), may hold values from -80 to 80, as said below
- page_table: int32 [32, 4], replicated, may hold values from 0 to 7, as said below
- owner_index: int32 [32], replicated, may hold values from 0 to 7
- suffix_lengths: int32 [8, 4], P('store'), may hold values from 1 to 128, 384 in all within a row
Outputs:
- attended: bfloat16 [4096, 8192], P(('store', 'tensor'))
The draws below stay inside these ranges and needn't reach their ends.
Inputs may be any that keep to these rules, and one draw needn't show every extreme that they name: `prefix_pool`: pool entries; the key halves of a few pages can be large. `page_table`: each row holds 4 distinct slots.
All inputs are finite; a program needn't handle non-finite values.
Results may differ from the reference program's by a relative error of at most 0.033.
Values may be sent and summed in bfloat16 or wider, within the bound.
A program may use at most 128 MiB of HBM per device.

```python
import math
import jax
import jax.numpy as jnp
import numpy as np
from jax import lax

D = 8192
HD = 128
HEADS_DEV = 2
PAGE = 16
PAGES_DEV = 4
SLAB = 128
SLABS = 4
HEADS = 64
KV_HEADS = 8
SLOTS = 8
PREFIX = 2048
ROWS = 512
N_STORE = 8
N_TENSOR = 32


def draw_prefix_pool(key, part):
    key = jax.random.fold_in(key, 11)
    first = jax.random.fold_in(key, 0)
    shape = (N_STORE, N_TENSOR * SLOTS, KV_HEADS, PAGE, 2 * HD)
    values = jnp.clip(jax.random.normal(first, shape, jnp.float32), -6.0, 6.0)
    return values.astype(jnp.bfloat16)


def draw_page_table(key, part):
    key = jax.random.fold_in(key, 12)
    first, second = jax.random.split(key)
    row_keys = jax.random.split(first, N_TENSOR)
    orders = jax.vmap(lambda one_key: jax.random.permutation(one_key, SLOTS))(row_keys)
    middle = jax.random.permutation(second, SLOTS - 2) + 1
    first_row = jnp.concatenate([jnp.array([SLOTS - 1, 0], jnp.int32), middle.astype(jnp.int32)])
    orders = orders.astype(jnp.int32).at[0].set(first_row)
    return orders[:, :PAGES_DEV].astype(jnp.int32)


def plant(values, own_key, smallest, top_value):
    longest = values.shape.index(max(values.shape))
    spots = []
    for shift in (0, 1):
        where = [jax.random.randint(jax.random.fold_in(own_key, axis), (), 0, length) for axis, length in enumerate(values.shape)]
        where[longest] = (where[longest] + shift) % values.shape[longest]
        spots.append(tuple(where))
    return values.at[spots[0]].set(smallest).at[spots[1]].set(top_value)


def steps_of(own_key, shape, cuts, smallest, largest):
    loudness = 1.0
    for dim, shards_of in cuts:
        draws = jax.random.uniform(jax.random.fold_in(jax.random.fold_in(own_key, 6), dim), (shards_of,), jnp.float32, smallest / len(cuts), largest / len(cuts))
        loudness = loudness * jnp.repeat(jnp.exp(draws), shape[dim] // shards_of).reshape((-1,) + (1,) * (len(shape) - 1 - dim))
    return loudness


def split_up(amount, total, reach, lean):
    weights = [(1 << 20) // math.isqrt(standing ** lean) + 1 for standing in range(2, amount + 1)]
    spare, counts = total - reach - (amount - 1), [1] * (amount - 1)
    while spare > 0:
        candidates = [i for i in range(amount - 1) if counts[i] < reach]
        mass, remaining = sum([weights[i] for i in candidates]), spare
        for i in candidates:
            more = min(reach - counts[i], max(1, remaining * weights[i] // mass), spare)
            counts[i] = counts[i] + more
            spare = spare - more
    return np.array([reach] + counts)


def uneven(rng, count, total, reach, skew):
    if count == 2:
        one = jax.random.randint(rng, (), max(1, total - reach), min(reach, total - 1) + 1)
        return jnp.stack([one, total - one])
    sizes = jnp.asarray(split_up(count, total, reach, skew), jnp.int32)
    twos = (count - 1) // 2
    source_of, sink = sizes[1:1 + 2 * twos:2], sizes[2:2 + 2 * twos:2]
    margin = jnp.minimum(source_of - 1, reach - sink)
    shifted = jax.random.randint(jax.random.fold_in(rng, 1), (twos,), 0, 1 << 20) % (margin + 1)
    sizes = sizes.at[1:1 + 2 * twos:2].set(source_of - shifted).at[2:2 + 2 * twos:2].set(sink + shifted)
    return sizes[jax.random.permutation(jax.random.fold_in(rng, 2), count)]


def bell_draw(rng, shape, width, limit, cuts=(), kind=jnp.bfloat16):
    level = steps_of(rng, shape, cuts, -0.22, 0.18) if cuts else 1.0
    values = jax.random.normal(rng, shape, jnp.float32) * width * level
    return jnp.minimum(jnp.maximum(values, -limit), limit).astype(kind)


def setup_inputs(seed: int = 0) -> dict:
    keys = jax.random.split(jax.random.key(seed), 9)
    return {
        "suffix_tokens": bell_draw(keys[0], (N_STORE * ROWS, D), 1.0, 6.0, ((0, 256),)),
        "q_weight": bell_draw(keys[1], (D, HEADS * HD), (D // 4) ** -0.5, 0.125, ((1, 32),)),
        "kv_weight": bell_draw(keys[2], (D, N_TENSOR, KV_HEADS, 2 * HD // N_TENSOR), D ** -0.5, 0.0625, ((1, 32),)),
        "out_weight": bell_draw(keys[3], (HEADS * HD, D), (2 * HD) ** -0.5, 0.375, ((0, 32),)),
        "prefix_pool": draw_prefix_pool(jax.random.fold_in(keys[8], 71), 0),
        "page_table": draw_page_table(jax.random.fold_in(keys[8], 71), 0),
        "owner_index": plant(jax.random.randint(keys[6], (N_TENSOR,), 0, N_STORE), jax.random.fold_in(keys[6], 1), 0, N_STORE - 1).astype(jnp.int32),
        "suffix_lengths": jax.vmap(lambda own: uneven(own, SLABS, 3 * SLABS * SLAB // 4, SLAB, 2))(jax.random.split(keys[7], N_STORE)).reshape((N_STORE, SLABS)).astype(jnp.int32),
    }


def rotate(values, positions):
    half_width = values.shape[-1] // 2
    frequency = 1000000.0 ** (-jnp.arange(half_width, dtype=jnp.float32) * 2.0 / values.shape[-1])
    angles = positions[:, None].astype(jnp.float32) * frequency[None, :]
    cosine = jnp.cos(angles)[:, None, :]
    sine = jnp.sin(angles)[:, None, :]
    lower_half = values[..., :half_width]
    upper_half = values[..., half_width:]
    return jnp.concatenate([lower_half * cosine - upper_half * sine, upper_half * cosine + lower_half * sine], -1)


def attend(queries, key_rows, value_rows, lengths, prefix_len, slab):
    query_count = queries.shape[1]
    scores = jnp.einsum('hsd,kd->hsk', queries.astype(jnp.float32), key_rows.astype(jnp.float32)) * (queries.shape[2] ** -0.5)
    query_index = jnp.arange(query_count, dtype=jnp.int32)
    key_index = jnp.arange(key_rows.shape[0], dtype=jnp.int32) - prefix_len
    same_slab = (key_index[None, :] // slab == query_index[:, None] // slab) & (key_index[None, :] <= query_index[:, None])
    allowed = (key_index[None, :] < 0) | same_slab
    scores = jnp.where(allowed[None], scores, -1e30)
    row_max = jnp.max(scores, -1, keepdims=True)
    exponent = jnp.exp(scores - row_max)
    denominator = jnp.sum(exponent, -1, keepdims=True)
    weights = (exponent / denominator).astype(jnp.bfloat16)
    mixed = jnp.einsum('hsk,kd->shd', weights.astype(jnp.float32), value_rows.astype(jnp.float32))
    slab_of = query_index // slab
    slab_limit = jnp.sum(jnp.where(slab_of[:, None] == jnp.arange(lengths.shape[0], dtype=jnp.int32)[None, :], lengths[None, :], 0), 1)
    query_live = (query_index % slab) < slab_limit
    return jnp.where(query_live[:, None, None], mixed, 0.0)


def reference(suffix_tokens, q_weight, kv_weight, out_weight, prefix_pool, page_table, owner_index, suffix_lengths):
    row_count = SLABS * SLAB
    key_heads = HEADS // 8
    slot_ids = (page_table + (jnp.arange(N_TENSOR, dtype=jnp.int32) * SLOTS)[:, None]).astype(jnp.int32)
    pages = prefix_pool[owner_index.astype(jnp.int32)[:, None], slot_ids]
    pages = pages.reshape(N_TENSOR * PAGES_DEV, key_heads, PAGE, 2 * HD)
    prefix = jnp.transpose(pages, (1, 0, 2, 3)).reshape(key_heads, PREFIX, 2 * HD)
    positions = PREFIX + jnp.arange(row_count, dtype=jnp.int32) % SLAB
    flat_kv = kv_weight.reshape(D, -1)
    outputs = []
    for group_index in range(N_STORE):
        tokens = suffix_tokens[group_index * row_count:(group_index + 1) * row_count]
        queries = jnp.dot(tokens, q_weight, preferred_element_type=jnp.float32).reshape(row_count, HEADS, HD)
        queries = rotate(queries, positions).astype(jnp.bfloat16)
        pairs = jnp.dot(tokens, flat_kv, preferred_element_type=jnp.float32).astype(jnp.bfloat16)
        pairs = pairs.reshape(row_count, N_TENSOR, key_heads, 2 * HD // N_TENSOR)
        pairs = jnp.transpose(pairs, (0, 2, 1, 3)).reshape(row_count, key_heads, 2 * HD)
        key_rows = rotate(pairs[:, :, :HD].astype(jnp.float32), positions).astype(jnp.bfloat16)
        value_rows = pairs[:, :, HD:]
        grouped = jnp.transpose(queries.reshape(row_count, key_heads, 8, HD), (1, 2, 0, 3))
        lengths = suffix_lengths[group_index]

        def one_head(items):
            head_queries, head_keys, head_values, head_prefix = items
            all_keys = jnp.concatenate([head_prefix[:, :HD], head_keys], 0)
            all_values = jnp.concatenate([head_prefix[:, HD:], head_values], 0)
            return attend(head_queries, all_keys, all_values, lengths, PREFIX, SLAB)

        mixed = lax.map(one_head, (grouped, jnp.transpose(key_rows, (1, 0, 2)), jnp.transpose(value_rows, (1, 0, 2)), prefix))
        heads_out = jnp.transpose(mixed, (1, 0, 2, 3)).reshape(row_count, HEADS * HD).astype(jnp.bfloat16)
        shares = jnp.transpose(heads_out.reshape(row_count, N_TENSOR, HEADS_DEV * HD), (1, 0, 2))
        blocks = out_weight.reshape(N_TENSOR, HEADS_DEV * HD, D)

        def add_share(running, items):
            share, block = items
            partial_value = jnp.dot(share, block, preferred_element_type=jnp.float32).astype(jnp.bfloat16)
            partial_value = lax.optimization_barrier(partial_value)
            return running + partial_value.astype(jnp.float32), None

        summed, unused = lax.scan(add_share, jnp.zeros((row_count, D), jnp.float32), (shares, blocks))
        outputs.append(summed.astype(jnp.bfloat16))
    return jnp.concatenate(outputs, 0)
```

```python
import jax
import jax.numpy as jnp
import numpy as np
from jax import lax
from jax.experimental import pallas as pl
from jax.experimental.pallas import tpu as pltpu
from jax.sharding import PartitionSpec as P

MESH = pl.DeviceIdType.MESH
F32 = jnp.float32
BF16 = jnp.bfloat16
HD = 128
SLAB = 128
ROW = 16
NZ = 8
PREFIX = 2048
NEG = -1e30
SCALE = 128 ** -0.5
PARTS = 2


def rope_tables():
    freq = np.float32(1000000.0) ** (-np.arange(HD // 2, dtype=np.float32) * np.float32(2.0) / np.float32(HD))
    pos = (PREFIX + np.arange(SLAB)).astype(np.float32)
    angles = (pos[:, None] * freq.astype(np.float32)[None, :]).astype(np.float32)
    cos = np.cos(angles.astype(np.float64)).astype(np.float32)
    sin = np.sin(angles.astype(np.float64)).astype(np.float32)
    by_row = np.stack([np.concatenate([cos, cos], 1), np.concatenate([-sin, sin], 1)])
    by_column = np.stack([cos.T, sin.T])
    return np.ascontiguousarray(by_row), np.ascontiguousarray(by_column)


def slab_order(zp):
    so, d = zp // 2, 2 * (zp % 2) - 1
    return [so, (so + 4 + d) % 4, (so + 4 - d) % 4, (so + 2) % 4]


def kernel(
    x_ref, qw_hbm, kvw_hbm, ow_hbm, pool_hbm, pt_ref, own_ref, len_ref, rope_ref, ropet_ref,
    out_ref,
    tok, qw, kvw, ow, pool, chosen, r1, sel, pb, kv0, kvs, kvr, lens, qs, ms, ls, accs, ho, hos,
    part, rb4, rb, rby,
    ssem, lsem, tsem, p1sem, p2sem, p3asem, p3bsem, p3csem, kvzsem, kvpsem, hosem, owsem, lensem,
    rb4sem, rbsem, rbysem,
):
    t = lax.axis_index("tensor")
    s = lax.axis_index("store")
    z, y, c = t // 4, lax.rem(t // 2, 2), lax.rem(t, 2)
    sx, yh = s // 2, lax.rem(s, 2)
    cols = x_ref.shape[1]
    wide = cols // PARTS
    parts = range(PARTS)
    cut = [pl.ds(g * wide, wide) for g in parts]

    def m8(v):
        return lax.rem(v + 16, 8)

    def tid(zz, yy, cc):
        return zz * 4 + yy * 2 + cc

    def tdev(zz, yy, cc):
        return {"tensor": tid(zz, yy, cc)}

    y4 = 2 * yh + y

    def ydev(step, cc):
        there = lax.rem(y4 + step + 4, 4)
        return {"store": sx * 2 + there // 2, "tensor": tid(z, lax.rem(there, 2), cc)}

    sib = tdev(z, y, 1 - c)
    ysend, yrecv = ydev(1 - 2 * c, c), ydev(2 * c - 1, c)
    plane = [((k, c), ydev(k, c)) for k in (1, 2, 3)] + [((k, 1 - c), ydev(k, 1 - c)) for k in range(4)]
    pending = []

    def send(src, dst, rsem, dev):
        copy = pltpu.make_async_remote_copy(
            src_ref=src, dst_ref=dst, send_sem=ssem.at[len(pending)], recv_sem=rsem,
            device_id=dev, device_id_type=MESH,
        )
        copy.start()
        pending.append(copy)

    def arrived(dst, rsem):
        pltpu.make_async_remote_copy(
            src_ref=dst, dst_ref=dst, send_sem=ssem.at[0], recv_sem=rsem,
            device_id=sib, device_id_type=MESH,
        ).wait_recv()

    own = tid(z, y, c)
    l_x = pltpu.make_async_copy(x_ref, tok.at[own], lsem.at[0])
    l_pool = pltpu.make_async_copy(pool_hbm, pool, lsem.at[1])
    l_kv = pltpu.make_async_copy(kvw_hbm, kvw, lsem.at[2])
    l_q = pltpu.make_async_copy(qw_hbm, qw, lsem.at[3])
    l_ow = pltpu.make_async_copy(ow_hbm, ow.at[0], lsem.at[4])
    l_x.start()
    l_pool.start()

    barrier = pltpu.get_barrier_semaphore()
    partners = [tdev(m8(z + k), y, c) for k in range(1, NZ)]
    partners += [{"store": lax.rem(s + k, 8)} for k in range(1, 8)]
    partners += [ysend, yrecv] + [ydev(k, 1 - c) for k in range(4)]
    for dev in partners:
        pl.semaphore_signal(barrier, inc=1, device_id=dev, device_id_type=MESH)

    l_pool.wait()
    for j in range(4):
        page = pool[pt_ref[j, t]]
        chosen[j, 0] = page[:, :, :HD]
        chosen[j, 1] = page[:, :, HD:]
    l_x.wait()
    pl.semaphore_wait(barrier, len(partners))
    l_kv.start()
    l_q.start()
    l_ow.start()

    def blk(b, h):
        return tok.at[b, :, cut[h]]

    def tsend(b, h, dev):
        send(blk(b, h), blk(b, h), tsem.at[h, b], dev)

    def twait(b, h):
        arrived(blk(b, h), tsem.at[h, b])

    up, down = tdev(m8(z + 1), y, c), tdev(m8(z - 1), y, c)
    step_dev = {1: up, -1: down}

    for g in parts:
        for dev in (up, down, ysend):
            tsend(own, g, dev)
    for k in range(1, 8):
        so = lax.rem(s + k, 8)
        send(chosen.at[so // 2, lax.rem(so, 2)], r1.at[s], p1sem.at[s], {"store": so})
    for g in parts:
        tsend(own, g, sib)
    r1[s] = chosen[sx, yh]
    for slab in range(8):
        lens[0, slab] = jnp.full((SLAB,), len_ref[0, slab % 4], jnp.int32).astype(F32)
    send(lens.at[0], lens.at[1], lensem.at[0], {"store": sx * 2 + 1 - yh})
    def z_step(k):
        for g in parts:
            turn = 1 - 2 * (g % 2)
            for d in (turn,) if k == 4 else (turn, -turn):
                b = tid(m8(z - d * k), y, c)
                twait(b, g)
                if k < 3 or (k == 3 and d == turn):
                    tsend(b, g, step_dev[d])
                tsend(b, g, ysend)
                tsend(b, g, sib)

    def y_step(k):
        for g in parts:
            for zz in [z] if k == 0 else [m8(z + 4)] if k == 4 else [m8(z - k), m8(z + k)]:
                b = tid(zz, 1 - y, c)
                twait(b, g)
                tsend(b, g, sib)

    def sib_wait(slab):
        for i in range(4):
            b = slab * 8 + i * 2 + 1 - c
            for g in parts:
                twait(b, g)

    so = z // 2
    dd = 2 * lax.rem(z, 2) - 1
    order = [so, lax.rem(so + 4 + dd, 4), lax.rem(so + 4 - dd, 4), lax.rem(so + 2, 4)]
    KC = 1024

    def rows_of(slabs, k):
        cs = pl.ds(pl.multiple_of(k * KC, KC), KC)
        rows = [tok[pl.ds(slab * 8, 8), :, cs].reshape(SLAB, KC) for slab in slabs]
        return rows[0] if len(rows) == 1 else jnp.concatenate(rows, 0)

    def kv_proj(*which):
        slabs = [order[i] for i in which]

        def body(k, acc):
            w = kvw[:, pl.ds(pl.multiple_of(k * KC, KC), KC)]
            return acc + lax.dot_general(
                rows_of(slabs, k), w, (((1,), (1,)), ((), ())), preferred_element_type=F32
            )

        res = lax.fori_loop(0, cols // KC, body, jnp.zeros((SLAB * len(slabs), 64), F32))
        return [res[i * SLAB : (i + 1) * SLAB].T for i in range(len(slabs))]

    def kv_send(m, first, second):
        for h in range(8):
            at = slice(h * 8, h * 8 + 8)
            kvs[m, h] = jnp.concatenate([first[at], second[at]], 0).astype(BF16)
        kvr[y4, c, m, z] = kvs[m, z]
        for k in range(1, NZ):
            zz = m8(z + k)
            send(kvs.at[m, zz], kvr.at[y4, c, m, z], kvzsem.at[m, z], tdev(zz, y, c))

    def kv_plane(m):
        for k in range(1, NZ):
            zz = m8(z + k)
            arrived(kvr.at[y4, c, m, zz], kvzsem.at[m, zz])
        for _, dev in plane:
            send(kvr.at[y4, c, m], kvr.at[y4, c, m], kvpsem.at[m, y4 * 2 + c], dev)

    def kv_wait(m):
        for (k, cc), _ in plane:
            yy = lax.rem(y4 + k, 4)
            arrived(kvr.at[yy, cc, m], kvpsem.at[m, yy * 2 + cc])

    def q_proj(*which):
        slabs = [order[i] for i in which]

        def body(k, acc):
            w = qw[pl.ds(pl.multiple_of(k * KC, KC), KC), :]
            return acc + jnp.dot(rows_of(slabs, k), w, preferred_element_type=F32)

        res = lax.fori_loop(0, cols // KC, body, jnp.zeros((SLAB * len(slabs), 2 * HD), F32))
        for i, slab in enumerate(slabs):
            for h in range(2):
                v = res[i * SLAB : (i + 1) * SLAB, h * HD : (h + 1) * HD]
                v = v * rope_ref[0] + pltpu.roll(v, HD // 2, 1) * rope_ref[1]
                qs[slab, pl.ds(h * SLAB, SLAB), :] = v.astype(BF16)

    def prefix_attn(i):
        slab = order[i]
        q = qs[slab]

        def body(x, carry):
            m, l, acc = carry
            keys = jnp.concatenate([pb[0, x, 0].reshape(256, HD), pb[1, x, 0].reshape(256, HD)], 0)
            vals = jnp.concatenate([pb[0, x, 1].reshape(256, HD), pb[1, x, 1].reshape(256, HD)], 0)
            sc = SCALE * lax.dot_general(
                q, keys, (((1,), (1,)), ((), ())), preferred_element_type=F32
            )
            m_new = jnp.maximum(m, jnp.max(sc, 1, keepdims=True))
            w = jnp.exp(sc - m_new)
            fix = jnp.exp(m - m_new)
            l = l * fix + jnp.sum(w, 1, keepdims=True)
            acc = acc * fix + jnp.dot(w.astype(BF16), vals, preferred_element_type=F32)
            return m_new, l, acc

        rows = 2 * SLAB
        m, l, acc = lax.fori_loop(
            0, 4, body,
            (jnp.full((rows, 1), NEG, F32), jnp.zeros((rows, 1), F32), jnp.zeros((rows, HD), F32)),
        )
        ms[slab] = jnp.broadcast_to(m, (rows, HD))
        ls[slab] = jnp.broadcast_to(l, (rows, HD))
        accs[slab] = acc

    ydevs = []
    for k in (1, 2, 3):
        there = lax.rem(y4 + k, 4)
        ydevs.append((ydev(k, c), there // 2, lax.rem(there, 2)))
    z_step(1)
    for k in range(1, 8):
        so = lax.rem(s + k, 8)
        arrived(r1.at[so], p1sem.at[so])
    sel[...] = r1[own_ref[t]]
    for k in range(1, NZ):
        zz = m8(z + k)
        send(sel.at[zz], pb.at[c, sx, yh, y, z], p2sem.at[z], tdev(zz, y, c))
    pb[c, sx, yh, y, z] = sel[z]
    y_step(0)
    z_step(2)
    for k in range(1, NZ):
        zz = m8(z + k)
        arrived(pb.at[c, sx, yh, y, zz], p2sem.at[zz])
    for dev, hh, yy in ydevs:
        send(pb.at[c, sx, yh, y], pb.at[c, sx, yh, y], p3asem.at[yh * 2 + y], dev)
    l_ow.wait()
    send(ow.at[0], ow.at[1], owsem.at[0], sib)
    y_step(1)
    z_step(3)
    for dev, hh, yy in ydevs:
        arrived(pb.at[c, sx, hh, yy], p3asem.at[hh * 2 + yy])
    for k in range(1, 4):
        xx = lax.rem(sx + k, 4)
        send(pb.at[c, sx], pb.at[c, sx], p3bsem.at[sx], {"store": xx * 2 + yh})
    y_step(2)
    l_kv.wait()
    l_q.wait()
    sib_wait(order[0])
    sib_wait(order[1])
    kv_send(0, *kv_proj(0, 1))
    q_proj(0, 1)
    for k in range(1, 4):
        xx = lax.rem(sx + k, 4)
        arrived(pb.at[c, xx], p3bsem.at[xx])
    send(pb.at[c], pb.at[c], p3csem.at[0], sib)
    z_step(4)
    y_step(3)
    arrived(pb.at[1 - c], p3csem.at[0])
    prefix_attn(0)
    sib_wait(order[2])
    kv0[...] = kv_proj(2)[0]
    y_step(4)
    q_proj(2)
    sib_wait(order[3])
    kv_send(1, kv0[...], kv_proj(3)[0])
    q_proj(3)
    kv_plane(0)
    prefix_attn(1)
    kv_plane(1)
    prefix_attn(2)
    prefix_attn(3)
    kv_wait(0)
    kv_wait(1)

    arrived(lens.at[1], lensem.at[0])
    row = lax.rem(lax.broadcasted_iota(jnp.int32, (2 * SLAB, 2 * SLAB), 0), SLAB)
    col = lax.broadcasted_iota(jnp.int32, (2 * SLAB, 2 * SLAB), 1)
    guest = lax.rem(row // ROW, 4) == 2 - y
    causal = (lax.rem(col, SLAB) <= row) & ((col >= SLAB) == guest)
    row, guest = row[:, :SLAB], guest[:, :SLAB]
    lane = lax.rem(lax.broadcasted_iota(jnp.int32, (HD, SLAB), 1) // ROW, 4)
    dim_y = lax.rem(lax.broadcasted_iota(jnp.int32, (HD, SLAB), 0) // 16, 2)
    key_guest = lane == 2 - dim_y
    orders = [slab_order(zp) for zp in range(NZ)]
    for slab in range(4):
        halves = []
        for hh in (yh, 1 - yh):
            pieces = []
            for zp in range(NZ):
                at = orders[zp].index(slab)
                m, low = at // 2, (at % 2) * 8
                for yy in range(2):
                    for cc in range(2):
                        pieces.append(kvr[2 * hh + yy, cc, m, zp].astype(F32)[low : low + 8])
            halves.append((jnp.concatenate(pieces[:16], 0), jnp.concatenate(pieces[16:], 0)))
        (k_here, v_here), (k_there, v_there) = halves
        keys, vals = [], []
        cos, sin = ropet_ref[0], ropet_ref[1]
        for x, y_ in (((k_here, v_here), (k_there, v_there)), ((k_there, v_there), (k_here, v_here))):
            kk = jnp.where(key_guest, y_[0], x[0])
            a, b = kk[: HD // 2], kk[HD // 2 :]
            keys.append(jnp.concatenate([a * cos - b * sin, b * cos + a * sin], 0).astype(BF16))
            vals.append(jnp.where(key_guest, y_[1], x[1]).astype(BF16))
        keys = jnp.concatenate(keys, 1)
        vals = jnp.concatenate(vals, 1)
        sc = SCALE * jnp.dot(qs[slab], keys, preferred_element_type=F32)
        sc = jnp.where(causal, sc, NEG)
        m_old = ms[slab]
        m_new = jnp.maximum(m_old, jnp.max(sc, 1, keepdims=True))
        w = jnp.where(causal, jnp.exp(sc - jnp.concatenate([m_new, m_new], 1)), 0.0)
        fix = jnp.exp(m_old - m_new)
        l = ls[slab] * fix + jnp.sum(w, 1, keepdims=True)
        acc = accs[slab] * fix + lax.dot_general(
            w.astype(BF16), vals, (((1,), (1,)), ((), ())), preferred_element_type=F32
        )
        live = jnp.where(guest, lens[1, slab : slab + 1], lens[0, slab : slab + 1])
        mixed = jnp.where(row.astype(F32) < live, acc / l, 0.0).astype(BF16)
        for i in range(8):
            rows16 = jnp.concatenate(
                [mixed[i * ROW : (i + 1) * ROW], mixed[SLAB + i * ROW : SLAB + (i + 1) * ROW]], 1
            )
            ho[i % 2, slab * 2 + i // 4, (i // 2) % 2] = rows16
        pair = pl.ds(slab * 2, 2)
        send(ho.at[1 - c, pair], hos.at[pair], hosem.at[slab], sib)
    arrived(ow.at[1], owsem.at[0])
    for slab in range(4):
        arrived(hos.at[pl.ds(slab * 2, 2)], hosem.at[slab])

    NC = 1024

    def out_proj(planes):
        a = jnp.concatenate([ho[c, zp].reshape(2 * ROW, 2 * HD) for zp in planes], 0)
        b = jnp.concatenate([hos[zp].reshape(2 * ROW, 2 * HD) for zp in planes], 0)

        for g in parts:

            def body(n, carry):
                at = pl.ds(pl.multiple_of(g * wide + n * NC, NC), NC)
                res = jnp.dot(a, ow[0, :, at], preferred_element_type=F32)
                res = res + jnp.dot(b, ow[1, :, at], preferred_element_type=F32)
                res = res.astype(BF16).reshape(len(planes), 2, ROW, NC)
                put = pl.ds(pl.multiple_of(n * NC, NC), NC)
                for i, zp in enumerate(planes):
                    part[g, zp, :, :, put] = res[i]
                return carry

            lax.fori_loop(0, wide // NC, body, 0)
        for zp in planes:
            for g in parts:
                send(part.at[g, zp, 1 - y], rby.at[g, zp], rbysem.at[g, zp], yrecv)

    def add(ref, *others):
        total = ref[...].astype(F32)
        for other in others:
            total = total + other[...].astype(F32)
        ref[...] = total.astype(BF16)

    def at(k):
        return m8(z + k)

    def by_wait(g, zp):
        arrived(rby.at[g, zp], rbysem.at[g, zp])

    out_proj([at(4), at(3), at(-3)])
    out_proj([at(2), at(-2), at(1), at(-1), z])
    for g in parts:
        turn = 1 - 2 * (g % 2)
        by_wait(g, at(4))
        add(part.at[g, at(4), y], rby.at[g, at(4)])
        send(part.at[g, at(4), y], rb4.at[g], rb4sem.at[g], step_dev[turn])
    for k in (3, 2, 1):
        for g in parts:
            turn = 1 - 2 * (g % 2)
            for d in (-turn, turn):
                zp = at(d * k)
                by_wait(g, zp)
                terms = [rby.at[g, zp]]
                if k == 3 and d == turn:
                    arrived(rb4.at[g], rb4sem.at[g])
                    terms.append(rb4.at[g])
                if k < 3:
                    arrived(rb.at[g, (1 - d) // 2, 2 - k], rbsem.at[g, (1 - d) // 2, 2 - k])
                    terms.append(rb.at[g, (1 - d) // 2, 2 - k])
                add(part.at[g, zp, y], *terms)
                i = (1 - d) // 2
                send(part.at[g, zp, y], rb.at[g, i, 3 - k], rbsem.at[g, i, 3 - k], step_dev[d])
    for g in parts:
        by_wait(g, z)
        for i in range(2):
            arrived(rb.at[g, i, 2], rbsem.at[g, i, 2])
        out_ref[:, cut[g]] = (
            part[g, z, y].astype(F32) + rby[g, z].astype(F32)
            + rb[g, 0, 2].astype(F32) + rb[g, 1, 2].astype(F32)
        ).astype(BF16)
    assert len(pending) <= 320
    for copy in pending:
        copy.wait_send()


def shards(x, qw, kvw, ow, pool, table, owner, lengths):
    cols = x.shape[1]
    wide = cols // PARTS
    kvw_t = jnp.transpose(kvw, (1, 2, 3, 0)).reshape(64, cols)
    rope, rope_t = rope_tables()
    any_ = pl.BlockSpec(memory_space=pl.ANY)
    smem = pl.BlockSpec(memory_space=pltpu.SMEM)
    vmem = pl.BlockSpec(memory_space=pltpu.VMEM)
    DMA = pltpu.SemaphoreType.DMA
    V = pltpu.VMEM
    scratch = [
        V((32, ROW, cols), BF16), V((cols, 256), BF16), V((64, cols), BF16), V((2, 256, cols), BF16),
        V((8, 8, 16, 256), BF16), V((4, 2, 8, 16, HD), BF16), V((8, 8, 16, HD), BF16), V((8, 16, HD), BF16),
        V((2, 4, 2, 2, NZ, 16, HD), BF16),
        V((64, SLAB), F32), V((2, 8, 16, SLAB), BF16), V((4, 2, 2, NZ, 16, SLAB), BF16), V((2, 8, SLAB), F32),
        V((4, 2 * SLAB, HD), BF16), V((4, 2 * SLAB, HD), F32), V((4, 2 * SLAB, HD), F32), V((4, 2 * SLAB, HD), F32),
        V((2, NZ, 2, ROW, 256), BF16), V((NZ, 2, ROW, 256), BF16),
        V((PARTS, NZ, 2, ROW, wide), BF16), V((PARTS, ROW, wide), BF16), V((PARTS, 2, 3, ROW, wide), BF16),
        V((PARTS, NZ, ROW, wide), BF16),
        DMA((320,)), DMA((5,)), DMA((PARTS, 32)), DMA((8,)), DMA((8,)), DMA((4,)), DMA((4,)), DMA((1,)),
        DMA((2, 8)), DMA((2, 8)), DMA((4,)), DMA((1,)), DMA((1,)),
        DMA((PARTS,)), DMA((PARTS, 2, 3)), DMA((PARTS, 8)),
    ]
    return pl.pallas_call(
        kernel,
        out_shape=jax.ShapeDtypeStruct((ROW, cols), BF16),
        in_specs=[any_] * 5 + [smem] * 3 + [vmem] * 2,
        out_specs=vmem,
        scratch_shapes=scratch,
        compiler_params=pltpu.CompilerParams(
            collective_id=0, has_side_effects=True, vmem_limit_bytes=56 * 1024 * 1024
        ),
    )(x, qw, kvw_t, ow, pool[0], jnp.transpose(table), owner, lengths, jnp.asarray(rope), jnp.asarray(rope_t))


def solution(mesh):
    placed = (
        P(("store", "tensor"), None),
        P(None, "tensor"),
        P(None, "tensor", None, None),
        P("tensor", None),
        P("store", "tensor", None, None, None),
        P(),
        P(),
        P("store", None),
    )
    return jax.shard_map(
        shards, mesh=mesh, in_specs=placed, out_specs=P(("store", "tensor"), None), check_vma=False
    )
```

```python
import jax
import jax.numpy as jnp
import numpy as np
from jax import lax
from jax.experimental import pallas as pl
from jax.experimental.pallas import tpu as pltpu
from jax.sharding import PartitionSpec as P

MESH = pl.DeviceIdType.MESH
F32 = jnp.float32
BF16 = jnp.bfloat16
HD = 128
SLAB = 128
ROW = 16
NZ = 8
PREFIX = 2048
NEG = -1e30
SCALE = 128 ** -0.5
PARTS = 2


def rope_tables():
    freq = np.float32(1000000.0) ** (-np.arange(HD // 2, dtype=np.float32) * np.float32(2.0) / np.float32(HD))
    pos = (PREFIX + np.arange(SLAB)).astype(np.float32)
    angles = (pos[:, None] * freq.astype(np.float32)[None, :]).astype(np.float32)
    cos = np.cos(angles.astype(np.float64)).astype(np.float32)
    sin = np.sin(angles.astype(np.float64)).astype(np.float32)
    by_row = np.stack([np.concatenate([cos, cos], 1), np.concatenate([-sin, sin], 1)])
    by_column = np.stack([cos.T, sin.T])
    return np.ascontiguousarray(by_row), np.ascontiguousarray(by_column)


def slab_order(zp):
    so, d = zp // 2, 2 * (zp % 2) - 1
    return [so, (so + 4 + d) % 4, (so + 4 - d) % 4, (so + 2) % 4]


def kernel(
    x_ref, qw_hbm, kvw_hbm, ow_hbm, pool_hbm, pt_ref, own_ref, len_ref, rope_ref, ropet_ref,
    out_ref,
    tok, qw, kvw, ow, pool, chosen, r1, sel, pb, kv0, kvs, kvr, lens, qs, ms, ls, accs, ho, hos,
    part, rb4, rb, rby,
    ssem, lsem, tsem, p1sem, p2sem, p3asem, p3bsem, p3csem, kvzsem, kvpsem, hosem, owsem, lensem,
    rb4sem, rbsem, rbysem,
):
    t = lax.axis_index("tensor")
    s = lax.axis_index("store")
    z, y, c = t // 4, lax.rem(t // 2, 2), lax.rem(t, 2)
    sx, yh = s // 2, lax.rem(s, 2)
    cols = x_ref.shape[1]
    wide = cols // PARTS
    parts = range(PARTS)
    cut = [pl.ds(g * wide, wide) for g in parts]

    def m8(v):
        return lax.rem(v + 16, 8)

    def tid(zz, yy, cc):
        return zz * 4 + yy * 2 + cc

    def tdev(zz, yy, cc):
        return {"tensor": tid(zz, yy, cc)}

    y4 = 2 * yh + y

    def ydev(step, cc):
        there = lax.rem(y4 + step + 4, 4)
        return {"store": sx * 2 + there // 2, "tensor": tid(z, lax.rem(there, 2), cc)}

    sib = tdev(z, y, 1 - c)
    ysend, yrecv = ydev(1 - 2 * c, c), ydev(2 * c - 1, c)
    plane = [((k, c), ydev(k, c)) for k in (1, 2, 3)] + [((k, 1 - c), ydev(k, 1 - c)) for k in range(4)]
    pending = []

    def send(src, dst, rsem, dev):
        copy = pltpu.make_async_remote_copy(
            src_ref=src, dst_ref=dst, send_sem=ssem.at[len(pending)], recv_sem=rsem,
            device_id=dev, device_id_type=MESH,
        )
        copy.start()
        pending.append(copy)

    def arrived(dst, rsem):
        pltpu.make_async_remote_copy(
            src_ref=dst, dst_ref=dst, send_sem=ssem.at[0], recv_sem=rsem,
            device_id=sib, device_id_type=MESH,
        ).wait_recv()

    own = tid(z, y, c)
    l_x = pltpu.make_async_copy(x_ref, tok.at[own], lsem.at[0])
    l_pool = pltpu.make_async_copy(pool_hbm, pool, lsem.at[1])
    l_kv = pltpu.make_async_copy(kvw_hbm, kvw, lsem.at[2])
    l_q = pltpu.make_async_copy(qw_hbm, qw, lsem.at[3])
    l_ow = pltpu.make_async_copy(ow_hbm, ow.at[0], lsem.at[4])
    l_x.start()
    l_pool.start()

    barrier = pltpu.get_barrier_semaphore()
    partners = [tdev(m8(z + k), y, c) for k in range(1, NZ)]
    partners += [{"store": lax.rem(s + k, 8)} for k in range(1, 8)]
    partners += [ysend, yrecv] + [ydev(k, 1 - c) for k in range(4)]
    for dev in partners:
        pl.semaphore_signal(barrier, inc=1, device_id=dev, device_id_type=MESH)

    l_pool.wait()
    for j in range(4):
        page = pool[pt_ref[j, t]]
        chosen[j, 0] = page[:, :, :HD]
        chosen[j, 1] = page[:, :, HD:]
    l_x.wait()
    pl.semaphore_wait(barrier, len(partners))
    l_kv.start()
    l_q.start()
    l_ow.start()

    def blk(b, h):
        return tok.at[b, :, cut[h]]

    def tsend(b, h, dev):
        send(blk(b, h), blk(b, h), tsem.at[h, b], dev)

    def twait(b, h):
        arrived(blk(b, h), tsem.at[h, b])

    up, down = tdev(m8(z + 1), y, c), tdev(m8(z - 1), y, c)
    step_dev = {1: up, -1: down}

    for g in parts:
        for dev in (up, down, ysend):
            tsend(own, g, dev)
    for k in range(1, 8):
        so = lax.rem(s + k, 8)
        send(chosen.at[so // 2, lax.rem(so, 2)], r1.at[s], p1sem.at[s], {"store": so})
    for g in parts:
        tsend(own, g, sib)
    r1[s] = chosen[sx, yh]
    for slab in range(8):
        lens[0, slab] = jnp.full((SLAB,), len_ref[0, slab % 4], jnp.int32).astype(F32)
    send(lens.at[0], lens.at[1], lensem.at[0], {"store": sx * 2 + 1 - yh})
    def z_step(k):
        for g in parts:
            turn = 1 - 2 * (g % 2)
            for d in (turn,) if k == 4 else (turn, -turn):
                b = tid(m8(z - d * k), y, c)
                twait(b, g)
                if k < 3 or (k == 3 and d == turn):
                    tsend(b, g, step_dev[d])
                tsend(b, g, ysend)
                tsend(b, g, sib)

    def y_step(k):
        for g in parts:
            for zz in [z] if k == 0 else [m8(z + 4)] if k == 4 else [m8(z - k), m8(z + k)]:
                b = tid(zz, 1 - y, c)
                twait(b, g)
                tsend(b, g, sib)

    def sib_wait(slab):
        for i in range(4):
            b = slab * 8 + i * 2 + 1 - c
            for g in parts:
                twait(b, g)

    so = z // 2
    dd = 2 * lax.rem(z, 2) - 1
    order = [so, lax.rem(so + 4 + dd, 4), lax.rem(so + 4 - dd, 4), lax.rem(so + 2, 4)]
    KC = 4096

    def rows_of(slabs, k):
        cs = pl.ds(pl.multiple_of(k * KC, KC), KC)
        rows = [tok[pl.ds(slab * 8, 8), :, cs].reshape(SLAB, KC) for slab in slabs]
        return rows[0] if len(rows) == 1 else jnp.concatenate(rows, 0)

    def kv_proj(*which):
        slabs = [order[i] for i in which]

        def body(k, acc):
            w = kvw[:, pl.ds(pl.multiple_of(k * KC, KC), KC)]
            return acc + lax.dot_general(
                rows_of(slabs, k), w, (((1,), (1,)), ((), ())), preferred_element_type=F32
            )

        res = lax.fori_loop(0, cols // KC, body, jnp.zeros((SLAB * len(slabs), 64), F32))
        return [res[i * SLAB : (i + 1) * SLAB].T for i in range(len(slabs))]

    def kv_send(m, first, second):
        for h in range(8):
            at = slice(h * 8, h * 8 + 8)
            kvs[m, h] = jnp.concatenate([first[at], second[at]], 0).astype(BF16)
        kvr[y4, c, m, z] = kvs[m, z]
        for k in range(1, NZ):
            zz = m8(z + k)
            send(kvs.at[m, zz], kvr.at[y4, c, m, z], kvzsem.at[m, z], tdev(zz, y, c))

    def kv_plane(m):
        for k in range(1, NZ):
            zz = m8(z + k)
            arrived(kvr.at[y4, c, m, zz], kvzsem.at[m, zz])
        for _, dev in plane:
            send(kvr.at[y4, c, m], kvr.at[y4, c, m], kvpsem.at[m, y4 * 2 + c], dev)

    def kv_wait(m):
        for (k, cc), _ in plane:
            yy = lax.rem(y4 + k, 4)
            arrived(kvr.at[yy, cc, m], kvpsem.at[m, yy * 2 + cc])

    def q_proj(*which):
        slabs = [order[i] for i in which]

        def body(k, acc):
            w = qw[pl.ds(pl.multiple_of(k * KC, KC), KC), :]
            return acc + jnp.dot(rows_of(slabs, k), w, preferred_element_type=F32)

        res = lax.fori_loop(0, cols // KC, body, jnp.zeros((SLAB * len(slabs), 2 * HD), F32))
        for i, slab in enumerate(slabs):
            for h in range(2):
                v = res[i * SLAB : (i + 1) * SLAB, h * HD : (h + 1) * HD]
                v = v * rope_ref[0] + pltpu.roll(v, HD // 2, 1) * rope_ref[1]
                qs[slab, pl.ds(h * SLAB, SLAB), :] = v.astype(BF16)

    def prefix_attn(i):
        slab = order[i]
        q = qs[slab]

        rows = 2 * SLAB
        scores, top = [], None
        for x in range(4):
            keys = jnp.concatenate([pb[0, x, 0].reshape(256, HD), pb[1, x, 0].reshape(256, HD)], 0)
            sc = lax.dot_general(q, keys, (((1,), (1,)), ((), ())), preferred_element_type=F32)
            scores.append(sc)
            part_max = sc[:, :HD]
            for i in range(1, 4):
                part_max = jnp.maximum(part_max, sc[:, i * HD : (i + 1) * HD])
            top = part_max if top is None else jnp.maximum(top, part_max)
        m = jnp.max(top, 1, keepdims=True) * SCALE
        l, acc = jnp.zeros((rows, HD), F32), jnp.zeros((rows, HD), F32)
        for x in range(4):
            vals = jnp.concatenate([pb[0, x, 1].reshape(256, HD), pb[1, x, 1].reshape(256, HD)], 0)
            w = jnp.exp(scores[x] * SCALE - m)
            for i in range(4):
                l = l + w[:, i * HD : (i + 1) * HD]
            acc = acc + jnp.dot(w.astype(BF16), vals, preferred_element_type=F32)
        l = jnp.sum(l, 1, keepdims=True)
        ms[slab] = jnp.broadcast_to(m, (rows, HD))
        ls[slab] = jnp.broadcast_to(l, (rows, HD))
        accs[slab] = acc

    ydevs = []
    for k in (1, 2, 3):
        there = lax.rem(y4 + k, 4)
        ydevs.append((ydev(k, c), there // 2, lax.rem(there, 2)))
    z_step(1)
    for k in range(1, 8):
        so = lax.rem(s + k, 8)
        arrived(r1.at[so], p1sem.at[so])
    sel[...] = r1[own_ref[t]]
    for k in range(1, NZ):
        zz = m8(z + k)
        send(sel.at[zz], pb.at[c, sx, yh, y, z], p2sem.at[z], tdev(zz, y, c))
    pb[c, sx, yh, y, z] = sel[z]
    y_step(0)
    z_step(2)
    for k in range(1, NZ):
        zz = m8(z + k)
        arrived(pb.at[c, sx, yh, y, zz], p2sem.at[zz])
    for dev, hh, yy in ydevs:
        send(pb.at[c, sx, yh, y], pb.at[c, sx, yh, y], p3asem.at[yh * 2 + y], dev)
    l_ow.wait()
    send(ow.at[0], ow.at[1], owsem.at[0], sib)
    y_step(1)
    z_step(3)
    for dev, hh, yy in ydevs:
        arrived(pb.at[c, sx, hh, yy], p3asem.at[hh * 2 + yy])
    for k in range(1, 4):
        xx = lax.rem(sx + k, 4)
        send(pb.at[c, sx], pb.at[c, sx], p3bsem.at[sx], {"store": xx * 2 + yh})
    y_step(2)
    l_kv.wait()
    l_q.wait()
    sib_wait(order[0])
    sib_wait(order[1])
    kv_send(0, *kv_proj(0, 1))
    q_proj(0, 1)
    for k in range(1, 4):
        xx = lax.rem(sx + k, 4)
        arrived(pb.at[c, xx], p3bsem.at[xx])
    send(pb.at[c], pb.at[c], p3csem.at[0], sib)
    z_step(4)
    y_step(3)
    arrived(pb.at[1 - c], p3csem.at[0])
    prefix_attn(0)
    sib_wait(order[2])
    kv0[...] = kv_proj(2)[0]
    y_step(4)
    q_proj(2)
    sib_wait(order[3])
    kv_send(1, kv0[...], kv_proj(3)[0])
    q_proj(3)
    kv_plane(0)
    prefix_attn(1)
    kv_plane(1)
    prefix_attn(2)
    prefix_attn(3)
    kv_wait(0)
    kv_wait(1)

    arrived(lens.at[1], lensem.at[0])
    row = lax.rem(lax.broadcasted_iota(jnp.int32, (2 * SLAB, SLAB), 0), SLAB)
    col = lax.broadcasted_iota(jnp.int32, (2 * SLAB, SLAB), 1)
    guest = lax.rem(row // ROW, 4) == 2 - y
    causal = col <= row
    lane = lax.rem(lax.broadcasted_iota(jnp.int32, (HD, SLAB), 1) // ROW, 4)
    dim_y = lax.rem(lax.broadcasted_iota(jnp.int32, (HD, SLAB), 0) // 16, 2)
    key_guest = lane == 2 - dim_y
    orders = [slab_order(zp) for zp in range(NZ)]
    for slab in range(4):
        halves = []
        for hh in (yh, 1 - yh):
            pieces = []
            for zp in range(NZ):
                at = orders[zp].index(slab)
                m, low = at // 2, (at % 2) * 8
                for yy in range(2):
                    for cc in range(2):
                        pieces.append(kvr[2 * hh + yy, cc, m, zp].astype(F32)[low : low + 8])
            halves.append((jnp.concatenate(pieces[:16], 0), jnp.concatenate(pieces[16:], 0)))
        (k_here, v_here), (k_there, v_there) = halves
        keys, vals = [], []
        cos, sin = ropet_ref[0], ropet_ref[1]
        for x, y_ in (((k_here, v_here), (k_there, v_there)), ((k_there, v_there), (k_here, v_here))):
            kk = jnp.where(key_guest, y_[0], x[0])
            a, b = kk[: HD // 2], kk[HD // 2 :]
            keys.append(jnp.concatenate([a * cos - b * sin, b * cos + a * sin], 0).astype(BF16))
            vals.append(jnp.where(key_guest, y_[1], x[1]).astype(BF16))
        q = qs[slab]
        sc = SCALE * jnp.where(
            guest,
            jnp.dot(q, keys[1], preferred_element_type=F32),
            jnp.dot(q, keys[0], preferred_element_type=F32),
        )
        sc = jnp.where(causal, sc, NEG)
        m_old = ms[slab]
        m_new = jnp.maximum(m_old, jnp.max(sc, 1, keepdims=True))
        w = jnp.where(causal, jnp.exp(sc - m_new), 0.0)
        fix = jnp.exp(m_old - m_new)
        l = ls[slab] * fix + jnp.sum(w, 1, keepdims=True)
        acc = accs[slab] * fix
        for part_w, v in ((jnp.where(guest, 0.0, w), vals[0]), (jnp.where(guest, w, 0.0), vals[1])):
            acc = acc + lax.dot_general(
                part_w.astype(BF16), v, (((1,), (1,)), ((), ())), preferred_element_type=F32
            )
        live = jnp.where(guest, lens[1, slab : slab + 1], lens[0, slab : slab + 1])
        mixed = jnp.where(row.astype(F32) < live, acc / l, 0.0).astype(BF16)
        for i in range(8):
            rows16 = jnp.concatenate(
                [mixed[i * ROW : (i + 1) * ROW], mixed[SLAB + i * ROW : SLAB + (i + 1) * ROW]], 1
            )
            ho[i % 2, slab * 2 + i // 4, (i // 2) % 2] = rows16
        pair = pl.ds(slab * 2, 2)
        send(ho.at[1 - c, pair], hos.at[pair], hosem.at[slab], sib)
    arrived(ow.at[1], owsem.at[0])
    for slab in range(4):
        arrived(hos.at[pl.ds(slab * 2, 2)], hosem.at[slab])

    NC = 1024

    def out_proj(planes):
        a = jnp.concatenate([ho[c, zp].reshape(2 * ROW, 2 * HD) for zp in planes], 0)
        b = jnp.concatenate([hos[zp].reshape(2 * ROW, 2 * HD) for zp in planes], 0)

        for g in parts:

            def body(n, carry):
                at = pl.ds(pl.multiple_of(g * wide + n * NC, NC), NC)
                res = jnp.dot(a, ow[0, :, at], preferred_element_type=F32)
                res = res + jnp.dot(b, ow[1, :, at], preferred_element_type=F32)
                res = res.astype(BF16).reshape(len(planes), 2, ROW, NC)
                put = pl.ds(pl.multiple_of(n * NC, NC), NC)
                for i, zp in enumerate(planes):
                    part[g, zp, :, :, put] = res[i]
                return carry

            lax.fori_loop(0, wide // NC, body, 0, unroll=True)
            if len(planes) == 3:
                for zp in planes:
                    send(part.at[g, zp, 1 - y], rby.at[g, zp], rbysem.at[g, zp], yrecv)
        if len(planes) > 3:
            for zp in planes:
                for g in parts:
                    send(part.at[g, zp, 1 - y], rby.at[g, zp], rbysem.at[g, zp], yrecv)

    def add(ref, *others):
        total = ref[...].astype(F32)
        for other in others:
            total = total + other[...].astype(F32)
        ref[...] = total.astype(BF16)

    def at(k):
        return m8(z + k)

    def by_wait(g, zp):
        arrived(rby.at[g, zp], rbysem.at[g, zp])

    out_proj([at(4), at(3), at(-3)])
    out_proj([at(2), at(-2), at(1), at(-1), z])
    for g in parts:
        turn = 1 - 2 * (g % 2)
        by_wait(g, at(4))
        add(part.at[g, at(4), y], rby.at[g, at(4)])
        send(part.at[g, at(4), y], rb4.at[g], rb4sem.at[g], step_dev[turn])
    for k in (3, 2, 1):
        for g in parts:
            turn = 1 - 2 * (g % 2)
            for d in (-turn, turn):
                zp = at(d * k)
                by_wait(g, zp)
                terms = [rby.at[g, zp]]
                if k == 3 and d == turn:
                    arrived(rb4.at[g], rb4sem.at[g])
                    terms.append(rb4.at[g])
                if k < 3:
                    arrived(rb.at[g, (1 - d) // 2, 2 - k], rbsem.at[g, (1 - d) // 2, 2 - k])
                    terms.append(rb.at[g, (1 - d) // 2, 2 - k])
                add(part.at[g, zp, y], *terms)
                i = (1 - d) // 2
                send(part.at[g, zp, y], rb.at[g, i, 3 - k], rbsem.at[g, i, 3 - k], step_dev[d])
    for g in parts:
        by_wait(g, z)
        for i in range(2):
            arrived(rb.at[g, i, 2], rbsem.at[g, i, 2])
        out_ref[:, cut[g]] = (
            part[g, z, y].astype(F32) + rby[g, z].astype(F32)
            + rb[g, 0, 2].astype(F32) + rb[g, 1, 2].astype(F32)
        ).astype(BF16)
    assert len(pending) <= 320
    for copy in pending:
        copy.wait_send()


def shards(x, qw, kvw, ow, pool, table, owner, lengths):
    cols = x.shape[1]
    wide = cols // PARTS
    kvw_t = jnp.transpose(kvw, (1, 2, 3, 0)).reshape(64, cols)
    rope, rope_t = rope_tables()
    any_ = pl.BlockSpec(memory_space=pl.ANY)
    smem = pl.BlockSpec(memory_space=pltpu.SMEM)
    vmem = pl.BlockSpec(memory_space=pltpu.VMEM)
    DMA = pltpu.SemaphoreType.DMA
    V = pltpu.VMEM
    scratch = [
        V((32, ROW, cols), BF16), V((cols, 256), BF16), V((64, cols), BF16), V((2, 256, cols), BF16),
        V((8, 8, 16, 256), BF16), V((4, 2, 8, 16, HD), BF16), V((8, 8, 16, HD), BF16), V((8, 16, HD), BF16),
        V((2, 4, 2, 2, NZ, 16, HD), BF16),
        V((64, SLAB), F32), V((2, 8, 16, SLAB), BF16), V((4, 2, 2, NZ, 16, SLAB), BF16), V((2, 8, SLAB), F32),
        V((4, 2 * SLAB, HD), BF16), V((4, 2 * SLAB, HD), F32), V((4, 2 * SLAB, HD), F32), V((4, 2 * SLAB, HD), F32),
        V((2, NZ, 2, ROW, 256), BF16), V((NZ, 2, ROW, 256), BF16),
        V((PARTS, NZ, 2, ROW, wide), BF16), V((PARTS, ROW, wide), BF16), V((PARTS, 2, 3, ROW, wide), BF16),
        V((PARTS, NZ, ROW, wide), BF16),
        DMA((320,)), DMA((5,)), DMA((PARTS, 32)), DMA((8,)), DMA((8,)), DMA((4,)), DMA((4,)), DMA((1,)),
        DMA((2, 8)), DMA((2, 8)), DMA((4,)), DMA((1,)), DMA((1,)),
        DMA((PARTS,)), DMA((PARTS, 2, 3)), DMA((PARTS, 8)),
    ]
    return pl.pallas_call(
        kernel,
        out_shape=jax.ShapeDtypeStruct((ROW, cols), BF16),
        in_specs=[any_] * 5 + [smem] * 3 + [vmem] * 2,
        out_specs=vmem,
        scratch_shapes=scratch,
        compiler_params=pltpu.CompilerParams(
            collective_id=0, has_side_effects=True, vmem_limit_bytes=56 * 1024 * 1024
        ),
    )(x, qw, kvw_t, ow, pool[0], jnp.transpose(table), owner, lengths, jnp.asarray(rope), jnp.asarray(rope_t))


def solution(mesh):
    placed = (
        P(("store", "tensor"), None),
        P(None, "tensor"),
        P(None, "tensor", None, None),
        P("tensor", None),
        P("store", "tensor", None, None, None),
        P(),
        P(),
        P("store", None),
    )
    return jax.shard_map(
        shards, mesh=mesh, in_specs=placed, out_specs=P(("store", "tensor"), None), check_vma=False
    )
```

```python
import jax
import jax.numpy as jnp
import numpy as np
from jax import lax
from jax.experimental import pallas as pl
from jax.experimental.pallas import tpu as pltpu
from jax.sharding import PartitionSpec as P

MESH = pl.DeviceIdType.MESH
F32 = jnp.float32
BF16 = jnp.bfloat16
HD = 128
SLAB = 128
ROW = 16
NZ = 8
PREFIX = 2048
NEG = -1e30
SCALE = 128 ** -0.5
PARTS = 2


def rope_tables():
    freq = np.float32(1000000.0) ** (-np.arange(HD // 2, dtype=np.float32) * np.float32(2.0) / np.float32(HD))
    pos = (PREFIX + np.arange(SLAB)).astype(np.float32)
    angles = (pos[:, None] * freq.astype(np.float32)[None, :]).astype(np.float32)
    cos = np.cos(angles.astype(np.float64)).astype(np.float32)
    sin = np.sin(angles.astype(np.float64)).astype(np.float32)
    by_row = np.stack([np.concatenate([cos, cos], 1), np.concatenate([-sin, sin], 1)])
    by_column = np.stack([cos.T, sin.T])
    return np.ascontiguousarray(by_row), np.ascontiguousarray(by_column)


def slab_order(zp):
    so, d = zp // 2, 2 * (zp % 2) - 1
    return [so, (so + 4 + d) % 4, (so + 4 - d) % 4, (so + 2) % 4]


def kernel(
    x_ref, qw_hbm, kvw_hbm, ow_hbm, pool_hbm, pt_ref, own_ref, len_ref, rope_ref, ropet_ref,
    out_ref,
    tok, qw, kvw, ow, pool, chosen, r1, sel, pb, kv0, kvs, kvr, lens, qs, ms, ls, accs, ho, hos,
    part, rb4, rb, rby,
    ssem, lsem, tsem, p1sem, p2sem, p3asem, p3bsem, p3csem, kvzsem, kvpsem, hosem, owsem, lensem,
    rb4sem, rbsem, rbysem,
):
    t = lax.axis_index("tensor")
    s = lax.axis_index("store")
    z, y, c = t // 4, lax.rem(t // 2, 2), lax.rem(t, 2)
    sx, yh = s // 2, lax.rem(s, 2)
    cols = x_ref.shape[1]
    wide = cols // PARTS
    parts = range(PARTS)
    cut = [pl.ds(g * wide, wide) for g in parts]

    def m8(v):
        return lax.rem(v + 16, 8)

    def tid(zz, yy, cc):
        return zz * 4 + yy * 2 + cc

    def tdev(zz, yy, cc):
        return {"tensor": tid(zz, yy, cc)}

    y4 = 2 * yh + y

    def ydev(step, cc):
        there = lax.rem(y4 + step + 4, 4)
        return {"store": sx * 2 + there // 2, "tensor": tid(z, lax.rem(there, 2), cc)}

    sib = tdev(z, y, 1 - c)
    ysend, yrecv = ydev(1 - 2 * c, c), ydev(2 * c - 1, c)
    plane = [((k, c), ydev(k, c)) for k in (1, 2, 3)] + [((k, 1 - c), ydev(k, 1 - c)) for k in range(4)]
    pending = []

    def send(src, dst, rsem, dev):
        copy = pltpu.make_async_remote_copy(
            src_ref=src, dst_ref=dst, send_sem=ssem.at[len(pending)], recv_sem=rsem,
            device_id=dev, device_id_type=MESH,
        )
        copy.start()
        pending.append(copy)

    def arrived(dst, rsem):
        pltpu.make_async_remote_copy(
            src_ref=dst, dst_ref=dst, send_sem=ssem.at[0], recv_sem=rsem,
            device_id=sib, device_id_type=MESH,
        ).wait_recv()

    own = tid(z, y, c)
    l_x = pltpu.make_async_copy(x_ref, tok.at[own], lsem.at[0])
    l_pool = pltpu.make_async_copy(pool_hbm, pool, lsem.at[1])
    l_kv = pltpu.make_async_copy(kvw_hbm, kvw, lsem.at[2])
    l_q = pltpu.make_async_copy(qw_hbm, qw, lsem.at[3])
    l_ow = pltpu.make_async_copy(ow_hbm, ow.at[0], lsem.at[4])
    l_x.start()
    l_pool.start()

    barrier = pltpu.get_barrier_semaphore()
    partners = [tdev(m8(z + k), y, c) for k in range(1, NZ)]
    partners += [{"store": lax.rem(s + k, 8)} for k in range(1, 8)]
    partners += [ysend, yrecv] + [ydev(k, 1 - c) for k in range(4)]
    for dev in partners:
        pl.semaphore_signal(barrier, inc=1, device_id=dev, device_id_type=MESH)

    l_pool.wait()
    for j in range(4):
        page = pool[pt_ref[j, t]]
        chosen[j, 0] = page[:, :, :HD]
        chosen[j, 1] = page[:, :, HD:]
    l_x.wait()
    pl.semaphore_wait(barrier, len(partners))
    l_kv.start()
    l_q.start()
    l_ow.start()

    def blk(b, h):
        return tok.at[b, :, cut[h]]

    def tsend(b, h, dev):
        send(blk(b, h), blk(b, h), tsem.at[h, b], dev)

    def twait(b, h):
        arrived(blk(b, h), tsem.at[h, b])

    up, down = tdev(m8(z + 1), y, c), tdev(m8(z - 1), y, c)
    step_dev = {1: up, -1: down}

    for g in parts:
        for dev in (up, down, ysend):
            tsend(own, g, dev)
    for k in range(1, 8):
        so = lax.rem(s + k, 8)
        send(chosen.at[so // 2, lax.rem(so, 2)], r1.at[s], p1sem.at[s], {"store": so})
    for g in parts:
        tsend(own, g, sib)
    r1[s] = chosen[sx, yh]
    for slab in range(8):
        lens[0, slab] = jnp.full((SLAB,), len_ref[0, slab % 4], jnp.int32).astype(F32)
    send(lens.at[0], lens.at[1], lensem.at[0], {"store": sx * 2 + 1 - yh})
    def z_step(k):
        for g in parts:
            turn = 1 - 2 * (g % 2)
            for d in (turn,) if k == 4 else (turn, -turn):
                b = tid(m8(z - d * k), y, c)
                twait(b, g)
                if k < 3 or (k == 3 and d == turn):
                    tsend(b, g, step_dev[d])
                tsend(b, g, ysend)
                tsend(b, g, sib)

    def y_step(k):
        for g in parts:
            for zz in [z] if k == 0 else [m8(z + 4)] if k == 4 else [m8(z - k), m8(z + k)]:
                b = tid(zz, 1 - y, c)
                twait(b, g)
                tsend(b, g, sib)

    def sib_wait(slab):
        for i in range(4):
            b = slab * 8 + i * 2 + 1 - c
            for g in parts:
                twait(b, g)

    so = z // 2
    dd = 2 * lax.rem(z, 2) - 1
    order = [so, lax.rem(so + 4 + dd, 4), lax.rem(so + 4 - dd, 4), lax.rem(so + 2, 4)]
    KC = 4096

    def rows_of(slabs, k):
        cs = pl.ds(pl.multiple_of(k * KC, KC), KC)
        rows = [tok[pl.ds(slab * 8, 8), :, cs].reshape(SLAB, KC) for slab in slabs]
        return rows[0] if len(rows) == 1 else jnp.concatenate(rows, 0)

    def kv_proj(*which):
        slabs = [order[i] for i in which]

        def body(k, acc):
            w = kvw[:, pl.ds(pl.multiple_of(k * KC, KC), KC)]
            return acc + lax.dot_general(
                rows_of(slabs, k), w, (((1,), (1,)), ((), ())), preferred_element_type=F32
            )

        res = lax.fori_loop(0, cols // KC, body, jnp.zeros((SLAB * len(slabs), 64), F32))
        return [res[i * SLAB : (i + 1) * SLAB].T for i in range(len(slabs))]

    def kv_send(m, first, second):
        for h in range(8):
            at = slice(h * 8, h * 8 + 8)
            kvs[m, h] = jnp.concatenate([first[at], second[at]], 0).astype(BF16)
        kvr[y4, c, m, z] = kvs[m, z]
        for k in range(1, NZ):
            zz = m8(z + k)
            send(kvs.at[m, zz], kvr.at[y4, c, m, z], kvzsem.at[m, z], tdev(zz, y, c))

    def kv_plane(m):
        for k in range(1, NZ):
            zz = m8(z + k)
            arrived(kvr.at[y4, c, m, zz], kvzsem.at[m, zz])
        for _, dev in plane:
            send(kvr.at[y4, c, m], kvr.at[y4, c, m], kvpsem.at[m, y4 * 2 + c], dev)

    def kv_wait(m):
        for (k, cc), _ in plane:
            yy = lax.rem(y4 + k, 4)
            arrived(kvr.at[yy, cc, m], kvpsem.at[m, yy * 2 + cc])

    def q_proj(*which):
        slabs = [order[i] for i in which]

        def body(k, acc):
            w = qw[pl.ds(pl.multiple_of(k * KC, KC), KC), :]
            return acc + jnp.dot(rows_of(slabs, k), w, preferred_element_type=F32)

        res = lax.fori_loop(0, cols // KC, body, jnp.zeros((SLAB * len(slabs), 2 * HD), F32))
        for i, slab in enumerate(slabs):
            for h in range(2):
                v = res[i * SLAB : (i + 1) * SLAB, h * HD : (h + 1) * HD]
                v = v * rope_ref[0] + pltpu.roll(v, HD // 2, 1) * rope_ref[1]
                qs[slab, pl.ds(h * SLAB, SLAB), :] = v.astype(BF16)

    def prefix_attn(i):
        slab = order[i]
        q = qs[slab]

        rows = 2 * SLAB
        scores, top = [], None
        for x in range(4):
            keys = jnp.concatenate([pb[0, x, 0].reshape(256, HD), pb[1, x, 0].reshape(256, HD)], 0)
            sc = lax.dot_general(q, keys, (((1,), (1,)), ((), ())), preferred_element_type=F32)
            scores.append(sc)
            part_max = sc[:, :HD]
            for i in range(1, 4):
                part_max = jnp.maximum(part_max, sc[:, i * HD : (i + 1) * HD])
            top = part_max if top is None else jnp.maximum(top, part_max)
        m = jnp.max(top, 1, keepdims=True) * SCALE
        l, acc = jnp.zeros((rows, HD), F32), jnp.zeros((rows, HD), F32)
        for x in range(4):
            vals = jnp.concatenate([pb[0, x, 1].reshape(256, HD), pb[1, x, 1].reshape(256, HD)], 0)
            w = jnp.exp(scores[x] * SCALE - m)
            for i in range(4):
                l = l + w[:, i * HD : (i + 1) * HD]
            acc = acc + jnp.dot(w.astype(BF16), vals, preferred_element_type=F32)
        l = jnp.sum(l, 1, keepdims=True)
        ms[slab] = jnp.broadcast_to(m, (rows, HD))
        ls[slab] = jnp.broadcast_to(l, (rows, HD))
        accs[slab] = acc

    ydevs = []
    for k in (1, 2, 3):
        there = lax.rem(y4 + k, 4)
        ydevs.append((ydev(k, c), there // 2, lax.rem(there, 2)))
    z_step(1)
    for k in range(1, 8):
        so = lax.rem(s + k, 8)
        arrived(r1.at[so], p1sem.at[so])
    sel[...] = r1[own_ref[t]]
    for k in range(1, NZ):
        zz = m8(z + k)
        send(sel.at[zz], pb.at[c, sx, yh, y, z], p2sem.at[z], tdev(zz, y, c))
    pb[c, sx, yh, y, z] = sel[z]
    y_step(0)
    z_step(2)
    y_step(1)
    for k in range(1, NZ):
        zz = m8(z + k)
        arrived(pb.at[c, sx, yh, y, zz], p2sem.at[zz])
    for dev, hh, yy in ydevs:
        send(pb.at[c, sx, yh, y], pb.at[c, sx, yh, y], p3asem.at[yh * 2 + y], dev)
    l_ow.wait()
    send(ow.at[0], ow.at[1], owsem.at[0], sib)
    z_step(3)
    y_step(2)
    for dev, hh, yy in ydevs:
        arrived(pb.at[c, sx, hh, yy], p3asem.at[hh * 2 + yy])
    for k in range(1, 4):
        xx = lax.rem(sx + k, 4)
        send(pb.at[c, sx], pb.at[c, sx], p3bsem.at[sx], {"store": xx * 2 + yh})
    l_kv.wait()
    l_q.wait()
    sib_wait(order[0])
    sib_wait(order[1])
    kv_send(0, *kv_proj(0, 1))
    q_proj(0, 1)
    z_step(4)
    y_step(3)
    for k in range(1, 4):
        xx = lax.rem(sx + k, 4)
        arrived(pb.at[c, xx], p3bsem.at[xx])
    send(pb.at[c], pb.at[c], p3csem.at[0], sib)
    sib_wait(order[2])
    kv0[...] = kv_proj(2)[0]
    y_step(4)
    q_proj(2)
    sib_wait(order[3])
    kv_send(1, kv0[...], kv_proj(3)[0])
    kv_plane(0)
    q_proj(3)
    arrived(pb.at[1 - c], p3csem.at[0])
    prefix_attn(0)
    kv_plane(1)
    prefix_attn(1)
    prefix_attn(2)
    prefix_attn(3)
    kv_wait(0)
    kv_wait(1)

    arrived(lens.at[1], lensem.at[0])
    row = lax.rem(lax.broadcasted_iota(jnp.int32, (2 * SLAB, SLAB), 0), SLAB)
    col = lax.broadcasted_iota(jnp.int32, (2 * SLAB, SLAB), 1)
    guest = lax.rem(row // ROW, 4) == 2 - y
    causal = col <= row
    lane = lax.rem(lax.broadcasted_iota(jnp.int32, (HD, SLAB), 1) // ROW, 4)
    dim_y = lax.rem(lax.broadcasted_iota(jnp.int32, (HD, SLAB), 0) // 16, 2)
    key_guest = lane == 2 - dim_y
    orders = [slab_order(zp) for zp in range(NZ)]
    for slab in range(4):
        halves = []
        for hh in (yh, 1 - yh):
            pieces = []
            for zp in range(NZ):
                at = orders[zp].index(slab)
                m, low = at // 2, (at % 2) * 8
                for yy in range(2):
                    for cc in range(2):
                        pieces.append(kvr[2 * hh + yy, cc, m, zp].astype(F32)[low : low + 8])
            halves.append((jnp.concatenate(pieces[:16], 0), jnp.concatenate(pieces[16:], 0)))
        (k_here, v_here), (k_there, v_there) = halves
        keys, vals = [], []
        cos, sin = ropet_ref[0], ropet_ref[1]
        for x, y_ in (((k_here, v_here), (k_there, v_there)), ((k_there, v_there), (k_here, v_here))):
            kk = jnp.where(key_guest, y_[0], x[0])
            a, b = kk[: HD // 2], kk[HD // 2 :]
            keys.append(jnp.concatenate([a * cos - b * sin, b * cos + a * sin], 0).astype(BF16))
            vals.append(jnp.where(key_guest, y_[1], x[1]).astype(BF16))
        q = qs[slab]
        sc = SCALE * jnp.where(
            guest,
            jnp.dot(q, keys[1], preferred_element_type=F32),
            jnp.dot(q, keys[0], preferred_element_type=F32),
        )
        sc = jnp.where(causal, sc, NEG)
        m_old = ms[slab]
        m_new = jnp.maximum(m_old, jnp.max(sc, 1, keepdims=True))
        w = jnp.where(causal, jnp.exp(sc - m_new), 0.0)
        fix = jnp.exp(m_old - m_new)
        l = ls[slab] * fix + jnp.sum(w, 1, keepdims=True)
        acc = accs[slab] * fix
        for part_w, v in ((jnp.where(guest, 0.0, w), vals[0]), (jnp.where(guest, w, 0.0), vals[1])):
            acc = acc + lax.dot_general(
                part_w.astype(BF16), v, (((1,), (1,)), ((), ())), preferred_element_type=F32
            )
        live = jnp.where(guest, lens[1, slab : slab + 1], lens[0, slab : slab + 1])
        mixed = jnp.where(row.astype(F32) < live, acc / l, 0.0).astype(BF16)
        for i in range(8):
            rows16 = jnp.concatenate(
                [mixed[i * ROW : (i + 1) * ROW], mixed[SLAB + i * ROW : SLAB + (i + 1) * ROW]], 1
            )
            ho[i % 2, slab * 2 + i // 4, (i // 2) % 2] = rows16
        pair = pl.ds(slab * 2, 2)
        send(ho.at[1 - c, pair], hos.at[pair], hosem.at[slab], sib)
    arrived(ow.at[1], owsem.at[0])
    for slab in range(4):
        arrived(hos.at[pl.ds(slab * 2, 2)], hosem.at[slab])

    NC = 1024

    def out_proj(planes):
        a = jnp.concatenate([ho[c, zp].reshape(2 * ROW, 2 * HD) for zp in planes], 0)
        b = jnp.concatenate([hos[zp].reshape(2 * ROW, 2 * HD) for zp in planes], 0)

        for g in parts:

            def body(n, carry):
                at = pl.ds(pl.multiple_of(g * wide + n * NC, NC), NC)
                res = jnp.dot(a, ow[0, :, at], preferred_element_type=F32)
                res = res + jnp.dot(b, ow[1, :, at], preferred_element_type=F32)
                res = res.astype(BF16).reshape(len(planes), 2, ROW, NC)
                put = pl.ds(pl.multiple_of(n * NC, NC), NC)
                for i, zp in enumerate(planes):
                    part[g, zp, :, :, put] = res[i]
                return carry

            lax.fori_loop(0, wide // NC, body, 0, unroll=True)
            if len(planes) == 3:
                for zp in planes:
                    send(part.at[g, zp, 1 - y], rby.at[g, zp], rbysem.at[g, zp], yrecv)
        if len(planes) > 3:
            for zp in planes:
                for g in parts:
                    send(part.at[g, zp, 1 - y], rby.at[g, zp], rbysem.at[g, zp], yrecv)

    def add(ref, *others):
        total = ref[...].astype(F32)
        for other in others:
            total = total + other[...].astype(F32)
        ref[...] = total.astype(BF16)

    def at(k):
        return m8(z + k)

    def by_wait(g, zp):
        arrived(rby.at[g, zp], rbysem.at[g, zp])

    out_proj([at(4), at(3), at(-3)])
    out_proj([at(2), at(-2), at(1), at(-1), z])
    for g in parts:
        turn = 1 - 2 * (g % 2)
        by_wait(g, at(4))
        add(part.at[g, at(4), y], rby.at[g, at(4)])
        send(part.at[g, at(4), y], rb4.at[g], rb4sem.at[g], step_dev[turn])
    for k in (3, 2, 1):
        for g in parts:
            turn = 1 - 2 * (g % 2)
            for d in (-turn, turn):
                zp = at(d * k)
                by_wait(g, zp)
                terms = [rby.at[g, zp]]
                if k == 3 and d == turn:
                    arrived(rb4.at[g], rb4sem.at[g])
                    terms.append(rb4.at[g])
                if k < 3:
                    arrived(rb.at[g, (1 - d) // 2, 2 - k], rbsem.at[g, (1 - d) // 2, 2 - k])
                    terms.append(rb.at[g, (1 - d) // 2, 2 - k])
                add(part.at[g, zp, y], *terms)
                i = (1 - d) // 2
                send(part.at[g, zp, y], rb.at[g, i, 3 - k], rbsem.at[g, i, 3 - k], step_dev[d])
    for g in parts:
        by_wait(g, z)
        for i in range(2):
            arrived(rb.at[g, i, 2], rbsem.at[g, i, 2])
        out_ref[:, cut[g]] = (
            part[g, z, y].astype(F32) + rby[g, z].astype(F32)
            + rb[g, 0, 2].astype(F32) + rb[g, 1, 2].astype(F32)
        ).astype(BF16)
    assert len(pending) <= 320
    for copy in pending:
        copy.wait_send()


def shards(x, qw, kvw, ow, pool, table, owner, lengths):
    cols = x.shape[1]
    wide = cols // PARTS
    kvw_t = jnp.transpose(kvw, (1, 2, 3, 0)).reshape(64, cols)
    rope, rope_t = rope_tables()
    any_ = pl.BlockSpec(memory_space=pl.ANY)
    smem = pl.BlockSpec(memory_space=pltpu.SMEM)
    vmem = pl.BlockSpec(memory_space=pltpu.VMEM)
    DMA = pltpu.SemaphoreType.DMA
    V = pltpu.VMEM
    scratch = [
        V((32, ROW, cols), BF16), V((cols, 256), BF16), V((64, cols), BF16), V((2, 256, cols), BF16),
        V((8, 8, 16, 256), BF16), V((4, 2, 8, 16, HD), BF16), V((8, 8, 16, HD), BF16), V((8, 16, HD), BF16),
        V((2, 4, 2, 2, NZ, 16, HD), BF16),
        V((64, SLAB), F32), V((2, 8, 16, SLAB), BF16), V((4, 2, 2, NZ, 16, SLAB), BF16), V((2, 8, SLAB), F32),
        V((4, 2 * SLAB, HD), BF16), V((4, 2 * SLAB, HD), F32), V((4, 2 * SLAB, HD), F32), V((4, 2 * SLAB, HD), F32),
        V((2, NZ, 2, ROW, 256), BF16), V((NZ, 2, ROW, 256), BF16),
        V((PARTS, NZ, 2, ROW, wide), BF16), V((PARTS, ROW, wide), BF16), V((PARTS, 2, 3, ROW, wide), BF16),
        V((PARTS, NZ, ROW, wide), BF16),
        DMA((320,)), DMA((5,)), DMA((PARTS, 32)), DMA((8,)), DMA((8,)), DMA((4,)), DMA((4,)), DMA((1,)),
        DMA((2, 8)), DMA((2, 8)), DMA((4,)), DMA((1,)), DMA((1,)),
        DMA((PARTS,)), DMA((PARTS, 2, 3)), DMA((PARTS, 8)),
    ]
    return pl.pallas_call(
        kernel,
        out_shape=jax.ShapeDtypeStruct((ROW, cols), BF16),
        in_specs=[any_] * 5 + [smem] * 3 + [vmem] * 2,
        out_specs=vmem,
        scratch_shapes=scratch,
        compiler_params=pltpu.CompilerParams(
            collective_id=0, has_side_effects=True, vmem_limit_bytes=56 * 1024 * 1024
        ),
    )(x, qw, kvw_t, ow, pool[0], jnp.transpose(table), owner, lengths, jnp.asarray(rope), jnp.asarray(rope_t))


def solution(mesh):
    placed = (
        P(("store", "tensor"), None),
        P(None, "tensor"),
        P(None, "tensor", None, None),
        P("tensor", None),
        P("store", "tensor", None, None, None),
        P(),
        P(),
        P("store", None),
    )
    return jax.shard_map(
        shards, mesh=mesh, in_specs=placed, out_specs=P(("store", "tensor"), None), check_vma=False
    )
```

```python
import jax
import jax.numpy as jnp
import numpy as np
from jax import lax
from jax.experimental import pallas as pl
from jax.experimental.pallas import tpu as pltpu
from jax.sharding import PartitionSpec as P

MESH = pl.DeviceIdType.MESH
F32 = jnp.float32
BF16 = jnp.bfloat16
HD = 128
SLAB = 128
ROW = 16
NZ = 8
PREFIX = 2048
NEG = -1e30
SCALE = 128 ** -0.5
PARTS = 2


def rope_tables():
    freq = np.float32(1000000.0) ** (-np.arange(HD // 2, dtype=np.float32) * np.float32(2.0) / np.float32(HD))
    pos = (PREFIX + np.arange(SLAB)).astype(np.float32)
    angles = (pos[:, None] * freq.astype(np.float32)[None, :]).astype(np.float32)
    cos = np.cos(angles.astype(np.float64)).astype(np.float32)
    sin = np.sin(angles.astype(np.float64)).astype(np.float32)
    by_row = np.stack([np.concatenate([cos, cos], 1), np.concatenate([-sin, sin], 1)])
    by_column = np.stack([cos.T, sin.T])
    return np.ascontiguousarray(by_row), np.ascontiguousarray(by_column)


def slab_order(zp):
    so, d = zp // 2, 2 * (zp % 2) - 1
    return [so, (so + 4 + d) % 4, (so + 4 - d) % 4, (so + 2) % 4]


def kernel(
    x_ref, qw_hbm, kvw_hbm, ow_hbm, pool_hbm, pt_ref, own_ref, len_ref, rope_ref, ropet_ref,
    out_ref,
    tok, qw, kvw, ow, pool, chosen, r1, sel, pb, kv0, kvs, kvr, lens, qs, ms, ls, accs, ho, hos,
    part, rb4, rb, rby,
    ssem, lsem, tsem, p1sem, p2sem, p3asem, p3bsem, p3csem, kvzsem, kvpsem, hosem, owsem, lensem,
    rb4sem, rbsem, rbysem,
):
    t = lax.axis_index("tensor")
    s = lax.axis_index("store")
    z, y, c = t // 4, lax.rem(t // 2, 2), lax.rem(t, 2)
    sx, yh = s // 2, lax.rem(s, 2)
    cols = x_ref.shape[1]
    wide = cols // PARTS
    parts = range(PARTS)
    cut = [pl.ds(g * wide, wide) for g in parts]

    def m8(v):
        return lax.rem(v + 16, 8)

    def tid(zz, yy, cc):
        return zz * 4 + yy * 2 + cc

    def tdev(zz, yy, cc):
        return {"tensor": tid(zz, yy, cc)}

    y4 = 2 * yh + y

    def ydev(step, cc):
        there = lax.rem(y4 + step + 4, 4)
        return {"store": sx * 2 + there // 2, "tensor": tid(z, lax.rem(there, 2), cc)}

    sib = tdev(z, y, 1 - c)
    ysend, yrecv = ydev(1 - 2 * c, c), ydev(2 * c - 1, c)
    plane = [((k, c), ydev(k, c)) for k in (1, 2, 3)] + [((k, 1 - c), ydev(k, 1 - c)) for k in range(4)]
    pending = []

    def send(src, dst, rsem, dev):
        copy = pltpu.make_async_remote_copy(
            src_ref=src, dst_ref=dst, send_sem=ssem.at[len(pending)], recv_sem=rsem,
            device_id=dev, device_id_type=MESH,
        )
        copy.start()
        pending.append(copy)

    def arrived(dst, rsem):
        pltpu.make_async_remote_copy(
            src_ref=dst, dst_ref=dst, send_sem=ssem.at[0], recv_sem=rsem,
            device_id=sib, device_id_type=MESH,
        ).wait_recv()

    own = tid(z, y, c)
    l_x = pltpu.make_async_copy(x_ref, tok.at[own], lsem.at[0])
    l_pool = pltpu.make_async_copy(pool_hbm, pool, lsem.at[1])
    l_kv = pltpu.make_async_copy(kvw_hbm, kvw, lsem.at[2])
    l_q = pltpu.make_async_copy(qw_hbm, qw, lsem.at[3])
    l_ow = pltpu.make_async_copy(ow_hbm, ow.at[0], lsem.at[4])
    l_x.start()
    l_pool.start()

    barrier = pltpu.get_barrier_semaphore()
    partners = [tdev(m8(z + k), y, c) for k in range(1, NZ)]
    partners += [{"store": lax.rem(s + k, 8)} for k in range(1, 8)]
    partners += [ysend, yrecv] + [ydev(k, 1 - c) for k in range(4)]
    for dev in partners:
        pl.semaphore_signal(barrier, inc=1, device_id=dev, device_id_type=MESH)

    l_pool.wait()
    for j in range(4):
        page = pool[pt_ref[j, t]]
        chosen[j, 0] = page[:, :, :HD]
        chosen[j, 1] = page[:, :, HD:]
    l_x.wait()
    pl.semaphore_wait(barrier, len(partners))
    l_kv.start()
    l_q.start()
    l_ow.start()

    def blk(b, h):
        return tok.at[b, :, cut[h]]

    def tsend(b, h, dev):
        send(blk(b, h), blk(b, h), tsem.at[h, b], dev)

    def twait(b, h):
        arrived(blk(b, h), tsem.at[h, b])

    up, down = tdev(m8(z + 1), y, c), tdev(m8(z - 1), y, c)
    step_dev = {1: up, -1: down}

    for g in parts:
        for dev in (up, down, ysend):
            tsend(own, g, dev)
    for k in range(1, 8):
        so = lax.rem(s + k, 8)
        send(chosen.at[so // 2, lax.rem(so, 2)], r1.at[s], p1sem.at[s], {"store": so})
    for g in parts:
        tsend(own, g, sib)
    r1[s] = chosen[sx, yh]
    for slab in range(8):
        lens[0, slab] = jnp.full((SLAB,), len_ref[0, slab % 4], jnp.int32).astype(F32)
    send(lens.at[0], lens.at[1], lensem.at[0], {"store": sx * 2 + 1 - yh})
    def z_step(k):
        for g in parts:
            turn = 1 - 2 * (g % 2)
            for d in (turn,) if k == 4 else (turn, -turn):
                b = tid(m8(z - d * k), y, c)
                twait(b, g)
                if k < 3 or (k == 3 and d == turn):
                    tsend(b, g, step_dev[d])
                tsend(b, g, ysend)
                tsend(b, g, sib)

    def y_step(k):
        for g in parts:
            for zz in [z] if k == 0 else [m8(z + 4)] if k == 4 else [m8(z - k), m8(z + k)]:
                b = tid(zz, 1 - y, c)
                twait(b, g)
                tsend(b, g, sib)

    def sib_wait(slab):
        for i in range(4):
            b = slab * 8 + i * 2 + 1 - c
            for g in parts:
                twait(b, g)

    so = z // 2
    dd = 2 * lax.rem(z, 2) - 1
    order = [so, lax.rem(so + 4 + dd, 4), lax.rem(so + 4 - dd, 4), lax.rem(so + 2, 4)]
    KC = 4096

    def rows_of(slabs, k):
        cs = pl.ds(pl.multiple_of(k * KC, KC), KC)
        rows = [tok[pl.ds(slab * 8, 8), :, cs].reshape(SLAB, KC) for slab in slabs]
        return rows[0] if len(rows) == 1 else jnp.concatenate(rows, 0)

    def kv_proj(*which):
        slabs = [order[i] for i in which]

        def body(k, acc):
            w = kvw[:, pl.ds(pl.multiple_of(k * KC, KC), KC)]
            return acc + lax.dot_general(
                rows_of(slabs, k), w, (((1,), (1,)), ((), ())), preferred_element_type=F32
            )

        res = lax.fori_loop(0, cols // KC, body, jnp.zeros((SLAB * len(slabs), 64), F32))
        return [res[i * SLAB : (i + 1) * SLAB].T for i in range(len(slabs))]

    def kv_send(m, first, second):
        for h in range(8):
            at = slice(h * 8, h * 8 + 8)
            kvs[m, h] = jnp.concatenate([first[at], second[at]], 0).astype(BF16)
        kvr[y4, c, m, z] = kvs[m, z]
        for k in range(1, NZ):
            zz = m8(z + k)
            send(kvs.at[m, zz], kvr.at[y4, c, m, z], kvzsem.at[m, z], tdev(zz, y, c))

    def kv_plane(m):
        for k in range(1, NZ):
            zz = m8(z + k)
            arrived(kvr.at[y4, c, m, zz], kvzsem.at[m, zz])
        for _, dev in plane:
            send(kvr.at[y4, c, m], kvr.at[y4, c, m], kvpsem.at[m, y4 * 2 + c], dev)

    def kv_wait(m):
        for (k, cc), _ in plane:
            yy = lax.rem(y4 + k, 4)
            arrived(kvr.at[yy, cc, m], kvpsem.at[m, yy * 2 + cc])

    def q_proj(*which):
        slabs = [order[i] for i in which]

        def body(k, acc):
            w = qw[pl.ds(pl.multiple_of(k * KC, KC), KC), :]
            return acc + jnp.dot(rows_of(slabs, k), w, preferred_element_type=F32)

        res = lax.fori_loop(0, cols // KC, body, jnp.zeros((SLAB * len(slabs), 2 * HD), F32))
        for i, slab in enumerate(slabs):
            for h in range(2):
                v = res[i * SLAB : (i + 1) * SLAB, h * HD : (h + 1) * HD]
                v = v * rope_ref[0] + pltpu.roll(v, HD // 2, 1) * rope_ref[1]
                qs[slab, pl.ds(h * SLAB, SLAB), :] = v.astype(BF16)

    def prefix_attn(i):
        slab = order[i]
        q = qs[slab]

        rows = 2 * SLAB
        scores, top = [], None
        for x in range(4):
            keys = jnp.concatenate([pb[0, x, 0].reshape(256, HD), pb[1, x, 0].reshape(256, HD)], 0)
            sc = lax.dot_general(q, keys, (((1,), (1,)), ((), ())), preferred_element_type=F32)
            scores.append(sc)
            part_max = sc[:, :HD]
            for i in range(1, 4):
                part_max = jnp.maximum(part_max, sc[:, i * HD : (i + 1) * HD])
            top = part_max if top is None else jnp.maximum(top, part_max)
        m = jnp.max(top, 1, keepdims=True) * SCALE
        l, acc = jnp.zeros((rows, HD), F32), jnp.zeros((rows, HD), F32)
        for x in range(4):
            vals = jnp.concatenate([pb[0, x, 1].reshape(256, HD), pb[1, x, 1].reshape(256, HD)], 0)
            w = jnp.exp(scores[x] * SCALE - m)
            for i in range(4):
                l = l + w[:, i * HD : (i + 1) * HD]
            acc = acc + jnp.dot(w.astype(BF16), vals, preferred_element_type=F32)
        l = jnp.sum(l, 1, keepdims=True)
        ms[slab] = jnp.broadcast_to(m, (rows, HD))
        ls[slab] = jnp.broadcast_to(l, (rows, HD))
        accs[slab] = acc

    ydevs = []
    for k in (1, 2, 3):
        there = lax.rem(y4 + k, 4)
        ydevs.append((ydev(k, c), there // 2, lax.rem(there, 2)))
    z_step(1)
    for k in range(1, 8):
        so = lax.rem(s + k, 8)
        arrived(r1.at[so], p1sem.at[so])
    sel[...] = r1[own_ref[t]]
    for k in range(1, NZ):
        zz = m8(z + k)
        send(sel.at[zz], pb.at[c, sx, yh, y, z], p2sem.at[z], tdev(zz, y, c))
    pb[c, sx, yh, y, z] = sel[z]
    y_step(0)
    z_step(2)
    y_step(1)
    for k in range(1, NZ):
        zz = m8(z + k)
        arrived(pb.at[c, sx, yh, y, zz], p2sem.at[zz])
    for dev, hh, yy in ydevs:
        send(pb.at[c, sx, yh, y], pb.at[c, sx, yh, y], p3asem.at[yh * 2 + y], dev)
    z_step(3)
    y_step(2)
    for dev, hh, yy in ydevs:
        arrived(pb.at[c, sx, hh, yy], p3asem.at[hh * 2 + yy])
    for k in range(1, 4):
        xx = lax.rem(sx + k, 4)
        send(pb.at[c, sx], pb.at[c, sx], p3bsem.at[sx], {"store": xx * 2 + yh})
    l_kv.wait()
    l_q.wait()
    sib_wait(order[0])
    sib_wait(order[1])
    kv_send(0, *kv_proj(0, 1))
    q_proj(0, 1)
    z_step(4)
    y_step(3)
    for k in range(1, 4):
        xx = lax.rem(sx + k, 4)
        arrived(pb.at[c, xx], p3bsem.at[xx])
    send(pb.at[c], pb.at[c], p3csem.at[0], sib)
    sib_wait(order[2])
    kv0[...] = kv_proj(2)[0]
    y_step(4)
    l_ow.wait()
    send(ow.at[0], ow.at[1], owsem.at[0], sib)
    q_proj(2)
    sib_wait(order[3])
    kv_send(1, kv0[...], kv_proj(3)[0])
    kv_plane(0)
    q_proj(3)
    arrived(pb.at[1 - c], p3csem.at[0])
    prefix_attn(0)
    kv_plane(1)
    prefix_attn(1)
    prefix_attn(2)
    prefix_attn(3)
    kv_wait(0)
    kv_wait(1)

    arrived(lens.at[1], lensem.at[0])
    row = lax.rem(lax.broadcasted_iota(jnp.int32, (2 * SLAB, SLAB), 0), SLAB)
    col = lax.broadcasted_iota(jnp.int32, (2 * SLAB, SLAB), 1)
    guest = lax.rem(row // ROW, 4) == 2 - y
    causal = col <= row
    lane = lax.rem(lax.broadcasted_iota(jnp.int32, (HD, SLAB), 1) // ROW, 4)
    dim_y = lax.rem(lax.broadcasted_iota(jnp.int32, (HD, SLAB), 0) // 16, 2)
    key_guest = lane == 2 - dim_y
    orders = [slab_order(zp) for zp in range(NZ)]
    for slab in range(4):
        halves = []
        for hh in (yh, 1 - yh):
            pieces = []
            for zp in range(NZ):
                at = orders[zp].index(slab)
                m, low = at // 2, (at % 2) * 8
                for yy in range(2):
                    for cc in range(2):
                        pieces.append(kvr[2 * hh + yy, cc, m, zp].astype(F32)[low : low + 8])
            halves.append((jnp.concatenate(pieces[:16], 0), jnp.concatenate(pieces[16:], 0)))
        (k_here, v_here), (k_there, v_there) = halves
        keys, vals = [], []
        cos, sin = ropet_ref[0], ropet_ref[1]
        for x, y_ in (((k_here, v_here), (k_there, v_there)), ((k_there, v_there), (k_here, v_here))):
            kk = jnp.where(key_guest, y_[0], x[0])
            a, b = kk[: HD // 2], kk[HD // 2 :]
            keys.append(jnp.concatenate([a * cos - b * sin, b * cos + a * sin], 0).astype(BF16))
            vals.append(jnp.where(key_guest, y_[1], x[1]).astype(BF16))
        q = qs[slab]
        sc = SCALE * jnp.where(
            guest,
            jnp.dot(q, keys[1], preferred_element_type=F32),
            jnp.dot(q, keys[0], preferred_element_type=F32),
        )
        sc = jnp.where(causal, sc, NEG)
        m_old = ms[slab]
        m_new = jnp.maximum(m_old, jnp.max(sc, 1, keepdims=True))
        w = jnp.where(causal, jnp.exp(sc - m_new), 0.0)
        fix = jnp.exp(m_old - m_new)
        l = ls[slab] * fix + jnp.sum(w, 1, keepdims=True)
        acc = accs[slab] * fix
        for part_w, v in ((jnp.where(guest, 0.0, w), vals[0]), (jnp.where(guest, w, 0.0), vals[1])):
            acc = acc + lax.dot_general(
                part_w.astype(BF16), v, (((1,), (1,)), ((), ())), preferred_element_type=F32
            )
        live = jnp.where(guest, lens[1, slab : slab + 1], lens[0, slab : slab + 1])
        mixed = jnp.where(row.astype(F32) < live, acc / l, 0.0).astype(BF16)
        for i in range(8):
            rows16 = jnp.concatenate(
                [mixed[i * ROW : (i + 1) * ROW], mixed[SLAB + i * ROW : SLAB + (i + 1) * ROW]], 1
            )
            ho[i % 2, slab * 2 + i // 4, (i // 2) % 2] = rows16
        pair = pl.ds(slab * 2, 2)
        send(ho.at[1 - c, pair], hos.at[pair], hosem.at[slab], sib)
    arrived(ow.at[1], owsem.at[0])
    for slab in range(4):
        arrived(hos.at[pl.ds(slab * 2, 2)], hosem.at[slab])

    NC = 1024

    def out_proj(planes):
        a = jnp.concatenate([ho[c, zp].reshape(2 * ROW, 2 * HD) for zp in planes], 0)
        b = jnp.concatenate([hos[zp].reshape(2 * ROW, 2 * HD) for zp in planes], 0)

        for g in parts:

            def body(n, carry):
                at = pl.ds(pl.multiple_of(g * wide + n * NC, NC), NC)
                res = jnp.dot(a, ow[0, :, at], preferred_element_type=F32)
                res = res + jnp.dot(b, ow[1, :, at], preferred_element_type=F32)
                res = res.astype(BF16).reshape(len(planes), 2, ROW, NC)
                put = pl.ds(pl.multiple_of(n * NC, NC), NC)
                for i, zp in enumerate(planes):
                    part[g, zp, :, :, put] = res[i]
                return carry

            lax.fori_loop(0, wide // NC, body, 0, unroll=True)
            if len(planes) == 3:
                for zp in planes:
                    send(part.at[g, zp, 1 - y], rby.at[g, zp], rbysem.at[g, zp], yrecv)
        if len(planes) > 3:
            for zp in planes:
                for g in parts:
                    send(part.at[g, zp, 1 - y], rby.at[g, zp], rbysem.at[g, zp], yrecv)

    def add(ref, *others):
        total = ref[...].astype(F32)
        for other in others:
            total = total + other[...].astype(F32)
        ref[...] = total.astype(BF16)

    def at(k):
        return m8(z + k)

    def by_wait(g, zp):
        arrived(rby.at[g, zp], rbysem.at[g, zp])

    out_proj([at(4), at(3), at(-3)])
    out_proj([at(2), at(-2), at(1), at(-1), z])
    for g in parts:
        turn = 1 - 2 * (g % 2)
        by_wait(g, at(4))
        add(part.at[g, at(4), y], rby.at[g, at(4)])
        send(part.at[g, at(4), y], rb4.at[g], rb4sem.at[g], step_dev[turn])
    for k in (3, 2, 1):
        for g in parts:
            turn = 1 - 2 * (g % 2)
            for d in (-turn, turn):
                zp = at(d * k)
                by_wait(g, zp)
                terms = [rby.at[g, zp]]
                if k == 3 and d == turn:
                    arrived(rb4.at[g], rb4sem.at[g])
                    terms.append(rb4.at[g])
                if k < 3:
                    arrived(rb.at[g, (1 - d) // 2, 2 - k], rbsem.at[g, (1 - d) // 2, 2 - k])
                    terms.append(rb.at[g, (1 - d) // 2, 2 - k])
                add(part.at[g, zp, y], *terms)
                i = (1 - d) // 2
                send(part.at[g, zp, y], rb.at[g, i, 3 - k], rbsem.at[g, i, 3 - k], step_dev[d])
    for g in parts:
        by_wait(g, z)
        for i in range(2):
            arrived(rb.at[g, i, 2], rbsem.at[g, i, 2])
        out_ref[:, cut[g]] = (
            part[g, z, y].astype(F32) + rby[g, z].astype(F32)
            + rb[g, 0, 2].astype(F32) + rb[g, 1, 2].astype(F32)
        ).astype(BF16)
    assert len(pending) <= 320
    for copy in pending:
        copy.wait_send()


def shards(x, qw, kvw, ow, pool, table, owner, lengths):
    cols = x.shape[1]
    wide = cols // PARTS
    kvw_t = jnp.transpose(kvw, (1, 2, 3, 0)).reshape(64, cols)
    rope, rope_t = rope_tables()
    any_ = pl.BlockSpec(memory_space=pl.ANY)
    smem = pl.BlockSpec(memory_space=pltpu.SMEM)
    vmem = pl.BlockSpec(memory_space=pltpu.VMEM)
    DMA = pltpu.SemaphoreType.DMA
    V = pltpu.VMEM
    scratch = [
        V((32, ROW, cols), BF16), V((cols, 256), BF16), V((64, cols), BF16), V((2, 256, cols), BF16),
        V((8, 8, 16, 256), BF16), V((4, 2, 8, 16, HD), BF16), V((8, 8, 16, HD), BF16), V((8, 16, HD), BF16),
        V((2, 4, 2, 2, NZ, 16, HD), BF16),
        V((64, SLAB), F32), V((2, 8, 16, SLAB), BF16), V((4, 2, 2, NZ, 16, SLAB), BF16), V((2, 8, SLAB), F32),
        V((4, 2 * SLAB, HD), BF16), V((4, 2 * SLAB, HD), F32), V((4, 2 * SLAB, HD), F32), V((4, 2 * SLAB, HD), F32),
        V((2, NZ, 2, ROW, 256), BF16), V((NZ, 2, ROW, 256), BF16),
        V((PARTS, NZ, 2, ROW, wide), BF16), V((PARTS, ROW, wide), BF16), V((PARTS, 2, 3, ROW, wide), BF16),
        V((PARTS, NZ, ROW, wide), BF16),
        DMA((320,)), DMA((5,)), DMA((PARTS, 32)), DMA((8,)), DMA((8,)), DMA((4,)), DMA((4,)), DMA((1,)),
        DMA((2, 8)), DMA((2, 8)), DMA((4,)), DMA((1,)), DMA((1,)),
        DMA((PARTS,)), DMA((PARTS, 2, 3)), DMA((PARTS, 8)),
    ]
    return pl.pallas_call(
        kernel,
        out_shape=jax.ShapeDtypeStruct((ROW, cols), BF16),
        in_specs=[any_] * 5 + [smem] * 3 + [vmem] * 2,
        out_specs=vmem,
        scratch_shapes=scratch,
        compiler_params=pltpu.CompilerParams(
            collective_id=0, has_side_effects=True, vmem_limit_bytes=56 * 1024 * 1024
        ),
    )(x, qw, kvw_t, ow, pool[0], jnp.transpose(table), owner, lengths, jnp.asarray(rope), jnp.asarray(rope_t))


def solution(mesh):
    placed = (
        P(("store", "tensor"), None),
        P(None, "tensor"),
        P(None, "tensor", None, None),
        P("tensor", None),
        P("store", "tensor", None, None, None),
        P(),
        P(),
        P("store", None),
    )
    return jax.shard_map(
        shards, mesh=mesh, in_specs=placed, out_specs=P(("store", "tensor"), None), check_vma=False
    )
```
